768 devices in a mesh: rep: 16 (over y, core), row: 48 (over x, z).
Axes of the slice: x: 4, y: 8, z: 12, core: 2. Of those that a mesh axis runs over, the one named last changes fastest.
Arguments:
- dense_act: bfloat16 [393216, 256], P(('rep', 'row')), may hold values from -6 to 6
- upstream: bfloat16 [393216, 1024], P(('rep', 'row')), may hold values from -6 to 6
- bottom_weight: bfloat16 [256, 128], replicated, may hold values from -0.375 to 0.375
- top_weight: bfloat16 [384, 1024], replicated, may hold values from -0.3125 to 0.3125
- hot_table: bfloat16 [512, 128], replicated, may hold values from -3 to 3
- cold_table: bfloat16 [196608, 128], P('row'), may hold values from -3 to 3
- hot_bags: int32 [393216, 8], P(('rep', 'row')), may hold values from 0 to 511
- cold_bags: int32 [393216, 16], P(('rep', 'row')), may hold values from 0 to 3071
- requests: int32 [16, 48, 48, 64], P('rep', 'row'), may hold values from 0 to 4095
Outputs:
- top_grad: float32 [384, 1024], replicated
- bottom_grad: float32 [256, 128], replicated
- hot_grad: float32 [512, 128], replicated
- cold_grad: float32 [196608, 128], P('row')
The draws below stay inside these ranges and needn't reach their ends.
All inputs are finite; a program needn't handle non-finite values.
Results may differ from the reference program's by a relative error of at most 0.015.
Values may be sent and summed in bfloat16 or wider, within the bound.
A program may use at most 32 MiB of HBM per device.

```python
import math
import jax
import jax.numpy as jnp
import numpy as np
from jax import lax

E = 128
D_BOT = 256
H_TOP = 1024
B_DEV = 512
L = 16
LH = 8
CAP = 64
ROWS_DEV = 4096
HOT = 512
BATCH = 393216
COLD = 196608
SLOTS = 3072
N_REP = 16
N_ROW = 48


def touch_ends(values, own_key, low, largest):
    extent = values.shape
    spot = [jax.random.randint(jax.random.fold_in(own_key, axis), (), 0, extent[axis]) for axis in range(len(extent))]
    values = values.at[tuple(spot)].set(low)
    longest = extent.index(max(extent))
    spot[longest] = (spot[longest] + 1) % extent[longest]
    return values.at[tuple(spot)].set(largest)


def block_scale(own_key, shape, pieces, smallest, largest):
    factor_of = 1.0
    for dim, parts in pieces:
        heights = jax.random.uniform(jax.random.fold_in(jax.random.fold_in(own_key, 6), dim), (parts,), jnp.float32, smallest / len(pieces), largest / len(pieces))
        factor_of = factor_of * jnp.repeat(jnp.exp(heights), shape[dim] // parts).reshape((-1,) + (1,) * (len(shape) - 1 - dim))
    return factor_of


def rank_table(amount, slope):
    weights = [(1 << 20) // math.isqrt(rank ** slope) + 1 for rank in range(1, amount + 1)]
    width = 1 + sum(weights) // (1 << 30)
    return np.cumsum(np.array([max(1, weight // width) for weight in weights]))


def ranked_ids(own_key, shape, number_of, skew):
    table = rank_table(number_of, skew)
    lot = jax.random.randint(jax.random.fold_in(own_key, 1), shape, 0, int(table[number_of - 1]))
    standing = jnp.searchsorted(jnp.asarray(table, jnp.int32), lot, side="right")
    return jax.random.permutation(jax.random.fold_in(own_key, 2), number_of)[standing].astype(jnp.int32)


def centred(own_key, extent, width, most, cuts=(), held_as=jnp.bfloat16):
    values = jax.random.normal(own_key, extent, jnp.float32) * width
    if len(cuts) > 0:
        values = block_scale(own_key, extent, cuts, -0.22, 0.18) * values
    return jnp.clip(values, min=-most, max=most).astype(held_as)


def setup_inputs(seed: int = 0) -> dict:
    key_list = jax.random.split(jax.random.key(seed), 10)
    dense_act = centred(key_list[0], (BATCH, D_BOT), 1.0, 6.0, ((0, 768),))
    upstream = centred(key_list[1], (BATCH, H_TOP), 1.0, 6.0, ((0, 768),))
    bottom_weight = centred(key_list[2], (D_BOT, E), D_BOT ** -0.5, 0.375)
    top_weight = centred(key_list[3], (3 * E, H_TOP), (3 * E) ** -0.5, 0.3125)
    hot_table = centred(key_list[4], (HOT, E), 0.5, 3.0)
    cold_table = centred(key_list[5], (COLD, E), 0.5, 3.0, ((0, 48),))
    hot_bags = touch_ends(ranked_ids(key_list[6], (BATCH, LH), HOT, 2), jax.random.fold_in(key_list[6], 3), 0, HOT - 1).astype(jnp.int32)
    cold_bags = touch_ends(ranked_ids(key_list[7], (BATCH, L), SLOTS, 1), jax.random.fold_in(key_list[7], 3), 0, SLOTS - 1).astype(jnp.int32)
    requests = touch_ends(jax.random.randint(key_list[8], (N_REP, N_ROW, N_ROW, CAP), 0, ROWS_DEV), jax.random.fold_in(key_list[8], 1), 0, ROWS_DEV - 1).astype(jnp.int32)
    return {"dense_act": dense_act, "upstream": upstream, "bottom_weight": bottom_weight, "top_weight": top_weight, "hot_table": hot_table, "cold_table": cold_table, "hot_bags": hot_bags, "cold_bags": cold_bags, "requests": requests}


def silu_slope(value):
    sigma = jax.nn.sigmoid(value)
    return sigma * (1.0 + value * (1.0 - sigma))


def reference(dense_act, upstream, bottom_weight, top_weight, hot_table, cold_table, hot_bags, cold_bags, requests):
    slot_count = N_ROW * CAP
    offsets = (jnp.arange(N_ROW, dtype=jnp.int32) * ROWS_DEV)[:, None]
    global_ids = (requests + offsets[None, None]).reshape(N_REP, N_ROW, slot_count).astype(jnp.int32)
    blocks = (dense_act.reshape(N_REP, N_ROW, B_DEV, D_BOT), upstream.reshape(N_REP, N_ROW, B_DEV, H_TOP),
              hot_bags.reshape(N_REP, N_ROW, B_DEV, LH), cold_bags.reshape(N_REP, N_ROW, B_DEV, L), global_ids)

    def step(carry, block):
        top_acc, bottom_acc, hot_acc, cold_acc = carry
        dense_rows, upper_rows, hot_index, cold_index, slot_ids = block
        fetched = cold_table[slot_ids]
        bottom_pre = jnp.dot(dense_rows, bottom_weight, preferred_element_type=jnp.float32)
        lower = jax.nn.silu(bottom_pre)
        cold_pool = jnp.sum(fetched[cold_index].astype(jnp.float32), axis=1)
        hot_pool = jnp.sum(hot_table[hot_index].astype(jnp.float32), axis=1)
        features = jnp.concatenate([lower, cold_pool, hot_pool], axis=1).astype(jnp.bfloat16)
        top_pre = jnp.dot(features, top_weight, preferred_element_type=jnp.float32)
        top_delta = (upper_rows.astype(jnp.float32) * silu_slope(top_pre)).astype(jnp.bfloat16)
        top_acc = top_acc + jnp.dot(features.T, top_delta, preferred_element_type=jnp.float32)
        feature_grad = jnp.dot(top_delta, top_weight.T, preferred_element_type=jnp.float32)
        lower_grad = feature_grad[:, :E]
        cold_back = feature_grad[:, E:2 * E]
        hot_back = feature_grad[:, 2 * E:]
        bottom_delta = (lower_grad * silu_slope(bottom_pre)).astype(jnp.bfloat16)
        bottom_acc = bottom_acc + jnp.dot(dense_rows.T, bottom_delta, preferred_element_type=jnp.float32)
        hot_terms = jnp.broadcast_to(hot_back[:, None, :], (B_DEV, LH, E)).reshape(B_DEV * LH, E)
        hot_acc = hot_acc + jax.ops.segment_sum(hot_terms, hot_index.reshape(-1), num_segments=HOT)
        cold_terms = jnp.broadcast_to(cold_back[:, None, :], (B_DEV, L, E)).reshape(B_DEV * L, E)
        slot_grad = jax.ops.segment_sum(cold_terms, cold_index.reshape(-1), num_segments=slot_count).astype(jnp.bfloat16)
        cold_acc = cold_acc.at[slot_ids].add(slot_grad.astype(jnp.float32))
        return (top_acc, bottom_acc, hot_acc, cold_acc), None

    def group(carry, group_blocks):
        top_acc, bottom_acc, hot_acc, cold_total = carry
        start = (top_acc, bottom_acc, hot_acc, jnp.zeros((ROWS_DEV * N_ROW, E), jnp.float32))
        inner, unused = lax.scan(step, start, group_blocks)
        rounded = lax.optimization_barrier(inner[3].astype(jnp.bfloat16))
        cold_total = cold_total + rounded.astype(jnp.float32)
        return (inner[0], inner[1], inner[2], cold_total), None

    init = (jnp.zeros((3 * E, H_TOP), jnp.float32), jnp.zeros((D_BOT, E), jnp.float32),
            jnp.zeros((HOT, E), jnp.float32), jnp.zeros((ROWS_DEV * N_ROW, E), jnp.float32))
    result, unused = lax.scan(group, init, blocks)
    return (result[0], result[1], result[2], result[3])
```

```python
import jax
import jax.numpy as jnp
from jax import lax
from jax.experimental import pallas as pl
from jax.experimental.pallas import tpu as pltpu
from jax.sharding import PartitionSpec as P

E = 128
D_BOT = 256
H_TOP = 1024
B_DEV = 512
L = 16
LH = 8
CAP = 64
ROWS_DEV = 4096
HOT = 512
N_ROW = 48
N_REP = 16
SLOTS = N_ROW * CAP
NX, NY, NZ, NC = 4, 8, 12, 2

W_BOTTOM = 3 * E * (H_TOP // E)
W_HOT = W_BOTTOM + D_BOT
W_USED = W_HOT + HOT
W_ROWS = 4096
W_C = W_ROWS // NC
W_X = W_C // NX
W_Y = W_X // NY
W_Z = 8

G_C = ROWS_DEV // NC
G_Y = G_C // NY

BF = jnp.bfloat16
F32 = jnp.float32
VMEM_LIMIT = 56 * 1024 * 1024


def vmem():
    return pl.BlockSpec(memory_space=pltpu.VMEM)


def remote(src, dst, send_sem, recv_sem, device):
    return pltpu.make_async_remote_copy(
        src_ref=src,
        dst_ref=dst,
        send_sem=send_sem,
        recv_sem=recv_sem,
        device_id=device,
        device_id_type=pl.DeviceIdType.MESH,
    )


def signal(sem, device):
    pl.semaphore_signal(sem, inc=1, device_id=device, device_id_type=pl.DeviceIdType.MESH)


def position():
    rep = lax.axis_index("rep")
    row = lax.axis_index("row")
    return rep, row


def silu_slope(value):
    sigma = jax.nn.sigmoid(value)
    return sigma * (1.0 + value * (1.0 - sigma))


def fetch_kernel(
    req_ref, table_ref, out_ref, ids_ref, ids_smem, table32, stage32, stage, req_send, req_recv,
    row_send, row_recv, local_sem,
):
    rep, me = position()
    barrier = pltpu.get_barrier_semaphore()

    def greet(k, carry):
        signal(barrier, (rep, lax.rem(me + k, N_ROW)))
        return carry

    lax.fori_loop(1, N_ROW, greet, 0)
    pl.semaphore_wait(barrier, N_ROW - 1)

    def req_copy(k):
        peer = lax.rem(me + k, N_ROW)
        return remote(
            req_ref.at[peer], ids_ref.at[me], req_send.at[k], req_recv.at[me], (rep, peer)
        )

    def ask(k, carry):
        req_copy(k).start()
        return carry

    lax.fori_loop(1, N_ROW, ask, 0)
    own = pltpu.make_async_copy(req_ref.at[me], ids_ref.at[me], local_sem)
    own.start()

    def widen(i, carry):
        rows = pl.ds(pl.multiple_of(i * 256, 256), 256)
        table32[rows, :] = table_ref[rows, :].astype(F32)
        return carry

    lax.fori_loop(0, ROWS_DEV // 256, widen, 0)
    own.wait()

    def asked(k, carry):
        peer = lax.rem(me + k, N_ROW)
        remote(
            req_ref.at[peer], ids_ref.at[peer], req_send.at[k], req_recv.at[peer], (rep, peer)
        ).wait_recv()
        req_copy(k).wait_send()
        return carry

    lax.fori_loop(1, N_ROW, asked, 0)
    read = pltpu.make_async_copy(ids_ref, ids_smem, local_sem)
    read.start()
    read.wait()

    def row_copy(k):
        peer = lax.rem(me + k, N_ROW)
        return remote(
            stage.at[peer], out_ref.at[me], row_send.at[k], row_recv.at[me], (rep, peer)
        )

    def pick(peer):
        for i in range(CAP):
            row = ids_smem[peer, 0, i]
            stage32[pl.ds(i, 1), :] = table32[pl.ds(row, 1), :]
        return stage32[...].astype(BF)

    def serve(k, carry):
        peer = lax.rem(me + k, N_ROW)
        stage[peer] = pick(peer)
        row_copy(k).start()
        return carry

    lax.fori_loop(1, N_ROW, serve, 0)
    out_ref[me] = pick(me)

    def served(k, carry):
        peer = lax.rem(me + k, N_ROW)
        remote(
            stage.at[peer], out_ref.at[peer], row_send.at[k], row_recv.at[peer], (rep, peer)
        ).wait_recv()
        row_copy(k).wait_send()
        return carry

    lax.fori_loop(1, N_ROW, served, 0)


def fetch(requests, table):
    return pl.pallas_call(
        fetch_kernel,
        out_shape=(
            jax.ShapeDtypeStruct((N_ROW, CAP, E), BF),
            jax.ShapeDtypeStruct((N_ROW, 1, 128), jnp.int32),
        ),
        in_specs=[vmem(), vmem()],
        out_specs=(vmem(), vmem()),
        scratch_shapes=[
            pltpu.SMEM((N_ROW, 1, 128), jnp.int32),
            pltpu.VMEM((ROWS_DEV, E), F32),
            pltpu.VMEM((CAP, E), F32),
            pltpu.VMEM((N_ROW, CAP, E), BF),
            pltpu.SemaphoreType.DMA((N_ROW,)),
            pltpu.SemaphoreType.DMA((N_ROW,)),
            pltpu.SemaphoreType.DMA((N_ROW,)),
            pltpu.SemaphoreType.DMA((N_ROW,)),
            pltpu.SemaphoreType.DMA,
        ],
        compiler_params=pltpu.CompilerParams(
            collective_id=0, has_side_effects=True, vmem_limit_bytes=VMEM_LIMIT
        ),
        name="fetch",
    )(requests, table)


def contract_first(a, b):
    return lax.dot_general(a, b, (((0,), (0,)), ((), ())), preferred_element_type=F32)


def contract_last(a, b):
    return lax.dot_general(a, b, (((1,), (1,)), ((), ())), preferred_element_type=F32)


def mlp_kernel(
    fetched_ref, cold_ref, hot_ref, dense_ref, up_ref, bw_ref, tw_ref, table_ref, slot_ref, w_ref,
    cold_counts, hot_counts, feats, feats_t, fgrad,
):
    low = lax.broadcasted_iota(jnp.int32, (128, 128), 0)

    def count(j, carry):
        lanes = pl.ds(pl.multiple_of(j * 128, 128), 128)
        ids = cold_ref[:, lanes]
        lo = ids & 127
        hi = ids >> 7
        word = (hi * 43) >> 8
        amount = jnp.left_shift(jnp.ones_like(hi), 5 * (hi - 6 * word))
        for w in range(4):
            key = jnp.where(word == w, lo, -1)
            total = jnp.zeros((128, 128), jnp.int32)
            for l in range(L):
                total += jnp.where(low == key[l : l + 1, :], amount[l : l + 1, :], 0)
            for f in range(6):
                slab = ((total >> (5 * f)) & 31).astype(F32).astype(BF)
                cold_counts[(6 * w + f) * 128 : (6 * w + f + 1) * 128, lanes] = slab
        ids = hot_ref[:, lanes]
        lo = ids & 127
        amount = jnp.left_shift(jnp.ones_like(ids), 4 * (ids >> 7))
        total = jnp.zeros((128, 128), jnp.int32)
        for l in range(LH):
            total += jnp.where(low == lo[l : l + 1, :], amount[l : l + 1, :], 0)
        for f in range(4):
            slab = ((total >> (4 * f)) & 15).astype(F32).astype(BF)
            hot_counts[f * 128 : (f + 1) * 128, lanes] = slab
        return carry

    lax.fori_loop(0, B_DEV // 128, count, 0)

    bottom_pre = jnp.dot(dense_ref[...], bw_ref[...], preferred_element_type=F32)
    lower = bottom_pre * jax.nn.sigmoid(bottom_pre)
    feats[:, 0:E] = lower.astype(BF)
    slope = silu_slope(bottom_pre)

    pool = contract_first(fetched_ref[...], cold_counts[...])
    feats[:, E : 2 * E] = pool.T.astype(BF)
    pool = contract_first(table_ref[...], hot_counts[...])
    feats[:, 2 * E : 3 * E] = pool.T.astype(BF)
    feats_t[...] = feats[...].astype(F32).T.astype(BF)

    fgrad[...] = jnp.zeros_like(fgrad)
    for h in range(H_TOP // 256):
        cols = slice(h * 256, (h + 1) * 256)
        weight = tw_ref[:, cols]
        pre = jnp.dot(feats[...], weight, preferred_element_type=F32)
        delta = (up_ref[:, cols].astype(F32) * silu_slope(pre)).astype(BF)
        top = jnp.dot(feats_t[...], delta, preferred_element_type=F32).astype(BF)
        w_ref[768 * h : 768 * h + 384, :] = top[:, 0:128]
        w_ref[768 * h + 384 : 768 * h + 768, :] = top[:, 128:256]
        fgrad[...] += contract_last(delta, weight)

    bottom_delta = (fgrad[:, 0:E] * slope).astype(BF)
    w_ref[W_BOTTOM:W_HOT, :] = contract_first(dense_ref[...], bottom_delta).astype(BF)
    hot_back = fgrad[:, 2 * E : 3 * E].astype(BF)
    w_ref[W_HOT:W_USED, :] = jnp.dot(
        hot_counts[...], hot_back, preferred_element_type=F32
    ).astype(BF)
    w_ref[W_USED:W_ROWS, :] = jnp.zeros((W_ROWS - W_USED, E), BF)
    cold_back = fgrad[:, E : 2 * E].astype(BF)
    for s in range(SLOTS // 512):
        rows = slice(s * 512, (s + 1) * 512)
        slot_ref[rows, :] = jnp.dot(
            cold_counts[rows, :], cold_back, preferred_element_type=F32
        ).astype(BF)


def mlp(fetched, cold_bags, hot_bags, dense, upstream, bottom_weight, top_weight, hot_table):
    return pl.pallas_call(
        mlp_kernel,
        out_shape=(
            jax.ShapeDtypeStruct((SLOTS, E), BF),
            jax.ShapeDtypeStruct((W_ROWS, E), BF),
        ),
        in_specs=[vmem()] * 8,
        out_specs=(vmem(), vmem()),
        scratch_shapes=[
            pltpu.VMEM((SLOTS, B_DEV), BF),
            pltpu.VMEM((HOT, B_DEV), BF),
            pltpu.VMEM((B_DEV, 3 * E), BF),
            pltpu.VMEM((3 * E, B_DEV), BF),
            pltpu.VMEM((B_DEV, 3 * E), F32),
        ],
        compiler_params=pltpu.CompilerParams(vmem_limit_bytes=VMEM_LIMIT),
        name="mlp",
    )(fetched, cold_bags, hot_bags, dense, upstream, bottom_weight, top_weight, hot_table)


def back_kernel(
    slot_ref, w_ref, out_ref, sum_ref, part_c, half, part_x, quarter, part_y, eighth, part_z,
    row_send, row_recv, c_sem, x_send, x_recv, y_send, y_recv, z_send, z_recv, local_sem,
):
    rep, me = position()
    y, core = rep // NC, lax.rem(rep, NC)
    x, z = me // NZ, lax.rem(me, NZ)
    sibling = (y * NC + 1 - core, me)
    barrier = pltpu.get_barrier_semaphore()

    def greet(k, carry):
        signal(barrier, (rep, lax.rem(me + k, N_ROW)))
        return carry

    signal(barrier, sibling)

    def greet_y(k, carry):
        signal(barrier, (lax.rem(y + k, NY) * NC + core, me))
        return carry

    lax.fori_loop(1, NY, greet_y, 0)
    lax.fori_loop(1, N_ROW, greet, 0)
    pl.semaphore_wait(barrier, N_ROW - 1 + NY - 1 + 1)

    def half_rows(c):
        return pl.ds(pl.multiple_of(c * W_C, W_C), W_C)

    to_core = remote(
        w_ref.at[half_rows(1 - core)], part_c, c_sem.at[0], c_sem.at[1], sibling
    )
    to_core.start()

    def row_copy(k):
        peer = lax.rem(me + k, N_ROW)
        return remote(
            slot_ref.at[peer], out_ref.at[me], row_send.at[k], row_recv.at[me], (rep, peer)
        )

    def send(k, carry):
        row_copy(k).start()
        return carry

    lax.fori_loop(1, N_ROW, send, 0)
    own = pltpu.make_async_copy(slot_ref.at[me], out_ref.at[me], local_sem)
    own.start()

    to_core.wait()

    def add_c(i, carry):
        rows = pl.ds(pl.multiple_of(i * 256, 256), 256)
        mine = pl.ds(pl.multiple_of(core * W_C + i * 256, 256), 256)
        half[rows, :] = (w_ref[mine, :].astype(F32) + part_c[rows, :].astype(F32)).astype(BF)
        return carry

    lax.fori_loop(0, W_C // 256, add_c, 0)

    copies = []
    for k in range(1, NX):
        px = lax.rem(x + k, NX)
        copies.append(
            remote(
                half.at[pl.ds(pl.multiple_of(px * W_X, W_X), W_X)], part_x.at[k - 1],
                x_send.at[k - 1], x_recv.at[k - 1], (rep, px * NZ + z),
            )
        )
        copies[-1].start()
    for copy in copies:
        copy.wait()
    total = half[pl.ds(pl.multiple_of(x * W_X, W_X), W_X), :].astype(F32)
    for k in range(1, NX):
        total += part_x[k - 1].astype(F32)
    quarter[...] = total.astype(BF)

    copies = []
    for k in range(1, NY):
        py = lax.rem(y + k, NY)
        copies.append(
            remote(
                quarter.at[pl.ds(pl.multiple_of(py * W_Y, W_Y), W_Y)], part_y.at[k - 1],
                y_send.at[k - 1], y_recv.at[k - 1], (py * NC + core, me),
            )
        )
        copies[-1].start()
    for copy in copies:
        copy.wait()
    total = quarter[pl.ds(pl.multiple_of(y * W_Y, W_Y), W_Y), :].astype(F32)
    for k in range(1, NY):
        total += part_y[k - 1].astype(F32)
    eighth[0:W_Y, :] = total
    eighth[W_Y : NZ * W_Z, :] = jnp.zeros((NZ * W_Z - W_Y, E), F32)

    copies = []
    for k in range(1, NZ):
        pz = lax.rem(z + k, NZ)
        copies.append(
            remote(
                eighth.at[pl.ds(pl.multiple_of(pz * W_Z, W_Z), W_Z)], part_z.at[k - 1],
                z_send.at[k - 1], z_recv.at[k - 1], (rep, x * NZ + pz),
            )
        )
        copies[-1].start()
    for copy in copies:
        copy.wait()
    total = eighth[pl.ds(pl.multiple_of(z * W_Z, W_Z), W_Z), :]
    for k in range(1, NZ):
        total += part_z[k - 1]
    sum_ref[...] = total

    own.wait()

    def sent(k, carry):
        peer = lax.rem(me + k, N_ROW)
        remote(
            slot_ref.at[peer], out_ref.at[peer], row_send.at[k], row_recv.at[peer], (rep, peer)
        ).wait_recv()
        row_copy(k).wait_send()
        return carry

    lax.fori_loop(1, N_ROW, sent, 0)


def back(slot_grad, w):
    dma = pltpu.SemaphoreType.DMA
    return pl.pallas_call(
        back_kernel,
        out_shape=(
            jax.ShapeDtypeStruct((N_ROW, CAP, E), BF),
            jax.ShapeDtypeStruct((W_Z, E), F32),
        ),
        in_specs=[vmem(), vmem()],
        out_specs=(vmem(), vmem()),
        scratch_shapes=[
            pltpu.VMEM((W_C, E), BF),
            pltpu.VMEM((W_C, E), BF),
            pltpu.VMEM((NX - 1, W_X, E), BF),
            pltpu.VMEM((W_X, E), BF),
            pltpu.VMEM((NY - 1, W_Y, E), BF),
            pltpu.VMEM((NZ * W_Z, E), F32),
            pltpu.VMEM((NZ - 1, W_Z, E), F32),
            dma((N_ROW,)),
            dma((N_ROW,)),
            dma((2,)),
            dma((NX - 1,)),
            dma((NX - 1,)),
            dma((NY - 1,)),
            dma((NY - 1,)),
            dma((NZ - 1,)),
            dma((NZ - 1,)),
            dma,
        ],
        compiler_params=pltpu.CompilerParams(
            collective_id=1, has_side_effects=True, vmem_limit_bytes=VMEM_LIMIT
        ),
        name="back",
    )(slot_grad, w)


def owner_kernel(ids_ref, arrived_ref, out_ref):
    def block(i, carry):
        rows = pl.multiple_of(i * 256, 256)
        index = lax.broadcasted_iota(jnp.int32, (256, SLOTS), 0) + rows
        hits = jnp.where(index == ids_ref[...], 1.0, 0.0).astype(BF)
        total = jnp.dot(hits, arrived_ref[...], preferred_element_type=F32)
        out_ref[pl.ds(rows, 256), :] = total.astype(BF)
        return carry

    lax.fori_loop(0, ROWS_DEV // 256, block, 0)


def owner(ids, arrived):
    return pl.pallas_call(
        owner_kernel,
        out_shape=jax.ShapeDtypeStruct((ROWS_DEV, E), BF),
        in_specs=[vmem(), vmem()],
        out_specs=vmem(),
        compiler_params=pltpu.CompilerParams(vmem_limit_bytes=VMEM_LIMIT),
        name="owner",
    )(ids, arrived)


def share_kernel(
    cold_ref, sum_ref, cold_out, w_out, got_c, mine, got_y, final, gath_z, w_y, gath_y, gath_x,
    c_send, c_recv, y_send, y_recv, a_send, a_recv, b_send, b_recv,
    wz_send, wz_recv, wy_send, wy_recv, wx_send, wx_recv, wc_sem,
):
    rep, me = position()
    y, core = rep // NC, lax.rem(rep, NC)
    x, z = me // NZ, lax.rem(me, NZ)
    sibling = (y * NC + 1 - core, me)
    barrier = pltpu.get_barrier_semaphore()

    def y_peer(k):
        return (lax.rem(y + k, NY) * NC + core, me)

    def x_peer(k):
        return (rep, lax.rem(x + k, NX) * NZ + z)

    def z_peer(k):
        return (rep, x * NZ + lax.rem(z + k, NZ))

    signal(barrier, sibling)
    for k in range(1, NY):
        signal(barrier, y_peer(k))
    for k in range(1, NX):
        signal(barrier, x_peer(k))
    for k in range(1, NZ):
        signal(barrier, z_peer(k))
    pl.semaphore_wait(barrier, 1 + NY - 1 + NX - 1 + NZ - 1)

    def g_rows(c, j):
        return pl.ds(pl.multiple_of(c * G_C + j * G_Y, G_Y), G_Y)

    to_core = []
    for k in range(1, NY + 1):
        j = lax.rem(y + k, NY)
        to_core.append(
            remote(
                cold_ref.at[g_rows(1 - core, j)], got_c.at[k - 1], c_send.at[k - 1],
                c_recv.at[k - 1], sibling,
            )
        )
        to_core[-1].start()
    gath_z[0] = sum_ref[...]
    over_z = []
    for k in range(1, NZ):
        over_z.append(
            remote(sum_ref, gath_z.at[k], wz_send.at[k - 1], wz_recv.at[k - 1], z_peer(k))
        )
        over_z[-1].start()

    over_y = []
    for k in range(1, NY + 1):
        j = lax.rem(y + k, NY)
        to_core[k - 1].wait_recv()
        total = cold_ref[g_rows(core, j), :].astype(F32) + got_c[k - 1].astype(F32)
        if k < NY:
            mine[k - 1] = total.astype(BF)
            over_y.append(
                remote(
                    mine.at[k - 1], got_y.at[k - 1], y_send.at[k - 1], y_recv.at[k - 1], y_peer(k)
                )
            )
            over_y[-1].start()

    for copy in over_z:
        copy.wait()

    def place(k, carry):
        owner_z = lax.rem(z - k + NZ, NZ)
        w_y[pl.ds(pl.multiple_of(owner_z * W_Z, W_Z), W_Z), :] = gath_z[k]
        return carry

    lax.fori_loop(0, NZ, place, 0)
    gath_y[y] = w_y[0:W_Y, :].astype(BF)
    w_over_y = []
    for k in range(1, NY):
        w_over_y.append(
            remote(gath_y.at[y], gath_y.at[y], wy_send.at[k - 1], wy_recv.at[k - 1], y_peer(k))
        )
        w_over_y[-1].start()

    for k in range(1, NY):
        over_y[k - 1].wait_recv()
        total += got_y[k - 1].astype(F32)
    final[...] = total.astype(BF)
    share_y = []
    for k in range(1, NY):
        share_y.append(
            remote(
                final, cold_out.at[g_rows(core, y)], a_send.at[k - 1], a_recv.at[k - 1], y_peer(k)
            )
        )
        share_y[-1].start()
    share_c = [
        remote(final, cold_out.at[g_rows(core, y)], b_send.at[0], b_recv.at[0], sibling)
    ]
    share_c[0].start()
    cold_out[g_rows(core, y), :] = final[...]

    for copy in w_over_y:
        copy.wait()
    w_over_x = []
    for k in range(1, NX):
        w_over_x.append(
            remote(gath_y, gath_x.at[x], wx_send.at[k - 1], wx_recv.at[k - 1], x_peer(k))
        )
        w_over_x[-1].start()
    gath_x[x] = gath_y[...]

    for k in range(1, NY):
        share_y[k - 1].wait_recv()
        j = lax.rem(y - k + NY, NY)
        rows = cold_out.at[g_rows(core, j)]
        share_c.append(remote(rows, rows, b_send.at[k], b_recv.at[k], sibling))
        share_c[-1].start()

    for copy in w_over_x:
        copy.wait()
    w_over_c = remote(gath_x, w_out.at[core], wc_sem.at[0], wc_sem.at[1], sibling)
    w_over_c.start()
    w_out[core] = gath_x[...]

    for copy in to_core + over_y + share_y:
        copy.wait_send()
    for copy in share_c:
        copy.wait()
    w_over_c.wait()


def share(cold, part):
    dma = pltpu.SemaphoreType.DMA
    return pl.pallas_call(
        share_kernel,
        out_shape=(
            jax.ShapeDtypeStruct((ROWS_DEV, E), BF),
            jax.ShapeDtypeStruct((NC, NX, NY, W_Y, E), BF),
        ),
        in_specs=[vmem(), vmem()],
        out_specs=(vmem(), vmem()),
        scratch_shapes=[
            pltpu.VMEM((NY, G_Y, E), BF),
            pltpu.VMEM((NY - 1, G_Y, E), BF),
            pltpu.VMEM((NY - 1, G_Y, E), BF),
            pltpu.VMEM((G_Y, E), BF),
            pltpu.VMEM((NZ, W_Z, E), F32),
            pltpu.VMEM((NZ * W_Z, E), F32),
            pltpu.VMEM((NY, W_Y, E), BF),
            pltpu.VMEM((NX, NY, W_Y, E), BF),
            dma((NY,)),
            dma((NY,)),
            dma((NY - 1,)),
            dma((NY - 1,)),
            dma((NY - 1,)),
            dma((NY - 1,)),
            dma((NY,)),
            dma((NY,)),
            dma((NZ - 1,)),
            dma((NZ - 1,)),
            dma((NY - 1,)),
            dma((NY - 1,)),
            dma((NX - 1,)),
            dma((NX - 1,)),
            dma((2,)),
        ],
        compiler_params=pltpu.CompilerParams(
            collective_id=2, has_side_effects=True, vmem_limit_bytes=VMEM_LIMIT
        ),
        name="share",
    )(cold, part)


def local(
    dense_act,
    upstream,
    bottom_weight,
    top_weight,
    hot_table,
    cold_table,
    hot_bags,
    cold_bags,
    requests,
):
    asked = jnp.pad(requests.reshape(N_ROW, 1, CAP), ((0, 0), (0, 0), (0, 128 - CAP)))
    fetched, ids = fetch(asked, cold_table)
    slot_grad, w = mlp(
        fetched.reshape(SLOTS, E), cold_bags.T, hot_bags.T, dense_act, upstream, bottom_weight,
        top_weight, hot_table,
    )
    arrived, part = back(slot_grad.reshape(N_ROW, CAP, E), w)
    owned = owner(ids[:, 0, :CAP].reshape(1, SLOTS), arrived.reshape(SLOTS, E))
    cold, summed = share(owned, part)
    cold_grad = cold.astype(F32)
    summed = summed.reshape(W_ROWS, E)
    top_grad = (
        summed[:W_BOTTOM]
        .reshape(H_TOP // E, 3 * E, E)
        .transpose(1, 0, 2)
        .reshape(3 * E, H_TOP)
        .astype(F32)
    )
    bottom_grad = summed[W_BOTTOM:W_HOT].astype(F32)
    hot_grad = summed[W_HOT:W_USED].astype(F32)
    return (top_grad, bottom_grad, hot_grad, cold_grad)


def solution(mesh):
    placed = (
        P(("rep", "row"), None),
        P(("rep", "row"), None),
        P(),
        P(),
        P(),
        P("row", None),
        P(("rep", "row"), None),
        P(("rep", "row"), None),
        P("rep", "row", None, None),
    )
    return jax.shard_map(
        local,
        mesh=mesh,
        in_specs=placed,
        out_specs=(P(), P(), P(), P("row", None)),
        check_vma=False,
    )
```

```python
import jax
import jax.numpy as jnp
from jax import lax
from jax.experimental import pallas as pl
from jax.experimental.pallas import tpu as pltpu
from jax.sharding import PartitionSpec as P

E = 128
D_BOT = 256
H_TOP = 1024
B_DEV = 512
L = 16
LH = 8
CAP = 64
ROWS_DEV = 4096
HOT = 512
N_ROW = 48
N_REP = 16
SLOTS = N_ROW * CAP
NX, NY, NZ, NC = 4, 8, 12, 2

W_BOTTOM = 3 * E * (H_TOP // E)
W_HOT = W_BOTTOM + D_BOT
W_USED = W_HOT + HOT
W_ROWS = 4096
W_C = W_ROWS // NC
W_X = W_C // NX
W_Y = W_X // NY
W_Z = 8

G_C = ROWS_DEV // NC
G_Y = G_C // NY

BF = jnp.bfloat16
F32 = jnp.float32
VMEM_LIMIT = 56 * 1024 * 1024


def vmem():
    return pl.BlockSpec(memory_space=pltpu.VMEM)


def remote(src, dst, send_sem, recv_sem, device):
    return pltpu.make_async_remote_copy(
        src_ref=src,
        dst_ref=dst,
        send_sem=send_sem,
        recv_sem=recv_sem,
        device_id=device,
        device_id_type=pl.DeviceIdType.MESH,
    )


def signal(sem, device):
    pl.semaphore_signal(sem, inc=1, device_id=device, device_id_type=pl.DeviceIdType.MESH)


def position():
    rep = lax.axis_index("rep")
    row = lax.axis_index("row")
    return rep, row


def silu_slope(value):
    sigma = jax.nn.sigmoid(value)
    return sigma * (1.0 + value * (1.0 - sigma))


def contract_first(a, b):
    return lax.dot_general(a, b, (((0,), (0,)), ((), ())), preferred_element_type=F32)


def contract_last(a, b):
    return lax.dot_general(a, b, (((1,), (1,)), ((), ())), preferred_element_type=F32)


def offset(k, core):
    dx = k % NX
    j = k // NX
    dz = (j + 1) // 2 if j % 2 else -(j // 2)
    return dx, dz * (1 - 2 * core)


def offset_of(k, core):
    dx = lax.rem(k, NX)
    j = lax.div(k, NX)
    odd = lax.rem(j, 2)
    dz = odd * lax.div(j + 1, 2) - (1 - odd) * lax.div(j, 2)
    return dx, dz * (1 - 2 * core)


def step_kernel(
    req_ref, cold_ref, hot_ref, bw_ref, table_any, dense_any, up_any, tw_any, hott_any,
    cold_out, w_out, rows_any, arr_any,
    req_pad, ids_v, ids_smem, table, table32, stage32, stage, fetched,
    dense_ref, up_ref, tw_ref, hott_ref, cold_counts, hot_counts, feats, feats_t, deltas, fgrad,
    slot, w_ref, arr_v, acc, cold_b,
    part_c, half, part_x, quarter, part_y, eighth, part_z, summed,
    got_c, mine, got_y, final, gath_z, w_y, gath_y, gath_x,
    load_sem, req_send, req_recv, row_send, row_recv, arr_send, arr_recv, arr_sem,
    wc, rx_send, rx_recv, ry_send, ry_recv, rz_send, rz_recv,
    c_send, c_recv, y_send, y_recv, a_send, a_recv, b_send, b_recv,
    wz_send, wz_recv, wy_send, wy_recv, wx_send, wx_recv, wc_sem,
):
    rep, me = position()
    y, core = rep // NC, lax.rem(rep, NC)
    x, z = me // NZ, lax.rem(me, NZ)
    sibling = (y * NC + 1 - core, me)

    def to(k):
        dx, dz = offset(k, core)
        return lax.rem(x + dx, NX) * NZ + lax.rem(z + dz + NZ, NZ)

    def y_peer(k):
        return (lax.rem(y + k, NY) * NC + core, me)

    def x_peer(k):
        return (rep, lax.rem(x + k, NX) * NZ + z)

    def z_peer(k):
        return (rep, x * NZ + lax.rem(z + k, NZ))

    loads = []
    for i, (src, dst) in enumerate(
        (
            (table_any, table), (dense_any, dense_ref), (up_any, up_ref), (tw_any, tw_ref),
            (hott_any, hott_ref),
        )
    ):
        loads.append(pltpu.make_async_copy(src, dst, load_sem.at[i]))
        loads[-1].start()

    barrier = pltpu.get_barrier_semaphore()
    for k in range(1, N_ROW):
        signal(barrier, (rep, to(k)))
    signal(barrier, sibling)
    for k in range(1, NY):
        signal(barrier, y_peer(k))
    req_pad[:, :, 0:CAP] = req_ref[...]
    req_pad[:, :, CAP:128] = jnp.zeros((N_ROW, 1, 128 - CAP), jnp.int32)
    pl.semaphore_wait(barrier, N_ROW - 1 + 1 + NY - 1)

    asks = [None]
    for k in range(1, N_ROW):
        peer = to(k)
        asks.append(
            remote(req_pad.at[peer], ids_v.at[k], req_send.at[k], req_recv.at[k], (rep, peer))
        )
        asks[-1].start()
    ids_v[0] = req_pad[me]

    loads[0].wait()

    def widen(i, carry):
        rows = pl.ds(pl.multiple_of(i * 256, 256), 256)
        table32[rows, :] = table[rows, :].astype(F32)
        return carry

    lax.fori_loop(0, ROWS_DEV // 256, widen, 0)

    low = lax.broadcasted_iota(jnp.int32, (128, 128), 0)

    def count(j, carry):
        lanes = pl.ds(pl.multiple_of(j * 128, 128), 128)
        ids = cold_ref[:, lanes]
        lo = ids & 127
        hi = ids >> 7
        word = (hi * 43) >> 8
        amount = jnp.left_shift(jnp.ones_like(hi), 5 * (hi - 6 * word))
        for w in range(4):
            key = jnp.where(word == w, lo, -1)
            total = jnp.zeros((128, 128), jnp.int32)
            for l in range(L):
                total += jnp.where(low == key[l : l + 1, :], amount[l : l + 1, :], 0)
            for f in range(6):
                slab = ((total >> (5 * f)) & 31).astype(F32).astype(BF)
                cold_counts[(6 * w + f) * 128 : (6 * w + f + 1) * 128, lanes] = slab
        ids = hot_ref[:, lanes]
        lo = ids & 127
        amount = jnp.left_shift(jnp.ones_like(ids), 4 * (ids >> 7))
        total = jnp.zeros((128, 128), jnp.int32)
        for l in range(LH):
            total += jnp.where(low == lo[l : l + 1, :], amount[l : l + 1, :], 0)
        for f in range(4):
            slab = ((total >> (4 * f)) & 15).astype(F32).astype(BF)
            hot_counts[f * 128 : (f + 1) * 128, lanes] = slab
        return carry

    lax.fori_loop(0, B_DEV // 256, count, 0)

    for k in range(1, N_ROW):
        asks[k].wait_recv()
    read = pltpu.make_async_copy(ids_v, ids_smem, load_sem.at[0])
    read.start()
    read.wait()

    def pick(k):
        for i in range(CAP):
            row = ids_smem[k, 0, i]
            stage32[pl.ds(i, 1), :] = table32[pl.ds(row, 1), :]
        stage[k] = stage32[...].astype(BF)

    def serve(k, carry):
        dx, dz = offset_of(k, core)
        peer = lax.rem(x - dx + NX, NX) * NZ + lax.rem(z - dz + NZ, NZ)
        pick(k)
        remote(
            stage.at[k], rows_any.at[me], row_send.at[k], row_recv.at[k], (rep, peer)
        ).start()
        return carry

    lax.fori_loop(1, N_ROW, serve, 0)
    pick(0)
    own = pltpu.make_async_copy(stage.at[0], rows_any.at[me], load_sem.at[0])
    own.start()

    lax.fori_loop(B_DEV // 256, B_DEV // 128, count, 0)
    loads[1].wait()
    bottom_pre = jnp.dot(dense_ref[...], bw_ref[...], preferred_element_type=F32)
    lower = bottom_pre * jax.nn.sigmoid(bottom_pre)
    feats[:, 0:E] = lower.astype(BF)
    slope = silu_slope(bottom_pre)
    fgrad[:, 0:E] = slope
    for i in range(2, 5):
        loads[i].wait()
    pool = contract_first(hott_ref[...], hot_counts[...])
    feats[:, 2 * E : 3 * E] = pool.T.astype(BF)

    own.wait()
    for k in range(1, N_ROW):
        owner_k = to(k)
        remote(
            stage.at[k], rows_any.at[owner_k], row_send.at[k], row_recv.at[k], (rep, owner_k)
        ).wait_recv()
    read = pltpu.make_async_copy(rows_any, fetched, load_sem.at[1])
    read.start()
    read.wait()

    pool = contract_first(fetched[...].reshape(SLOTS, E), cold_counts[...])
    feats[:, E : 2 * E] = pool.T.astype(BF)
    slope = fgrad[:, 0:E]
    for h in range(H_TOP // 256):
        cols = slice(h * 256, (h + 1) * 256)
        weight = tw_ref[:, cols]
        pre = jnp.dot(feats[...], weight, preferred_element_type=F32)
        delta = (up_ref[:, cols].astype(F32) * silu_slope(pre)).astype(BF)
        deltas[:, cols] = delta
        term = contract_last(delta, weight)
        if h == 0:
            fgrad[...] = term
        else:
            fgrad[...] += term
    cold_back = fgrad[:, E : 2 * E].astype(BF)
    for s in range(SLOTS // 512):
        total = jnp.dot(
            cold_counts[s * 512 : (s + 1) * 512, :], cold_back, preferred_element_type=F32
        )
        slot[8 * s : 8 * s + 8] = total.astype(BF).reshape(8, CAP, E)

    sends = [None]
    for k in range(1, N_ROW):
        peer = to(k)
        sends.append(
            remote(slot.at[peer], arr_any.at[k], arr_send.at[k], arr_recv.at[k], (rep, peer))
        )
        sends[-1].start()
    own = pltpu.make_async_copy(slot.at[me], arr_any.at[0], load_sem.at[0])
    own.start()

    feats_t[...] = feats[...].astype(F32).T.astype(BF)
    for h in range(H_TOP // 256):
        cols = slice(h * 256, (h + 1) * 256)
        top = jnp.dot(feats_t[...], deltas[:, cols], preferred_element_type=F32).astype(BF)
        w_ref[768 * h : 768 * h + 384, :] = top[:, 0:128]
        w_ref[768 * h + 384 : 768 * h + 768, :] = top[:, 128:256]
    bottom_delta = (fgrad[:, 0:E] * slope).astype(BF)
    w_ref[W_BOTTOM:W_HOT, :] = contract_first(dense_ref[...], bottom_delta).astype(BF)
    hot_back = fgrad[:, 2 * E : 3 * E].astype(BF)
    w_ref[W_HOT:W_USED, :] = jnp.dot(
        hot_counts[...], hot_back, preferred_element_type=F32
    ).astype(BF)
    w_ref[W_USED:W_ROWS, :] = jnp.zeros((W_ROWS - W_USED, E), BF)

    to_half = remote(
        w_ref.at[pl.ds(pl.multiple_of((1 - core) * W_C, W_C), W_C)], part_c, wc.at[0], wc.at[1],
        sibling,
    )
    to_half.start()

    lane = lax.broadcasted_iota(jnp.int32, (1, 128), 1)
    place512 = lax.broadcasted_iota(jnp.int32, (512, 256), 0)

    def arrive(g):
        for k in range(4 * g, 4 * g + 4):
            if k == 0:
                own.wait()
            else:
                sends[k].wait_recv()
        copy = pltpu.make_async_copy(arr_any.at[4 * g : 4 * g + 4], arr_v.at[g % 2], arr_sem.at[g % 2])
        copy.start()
        return copy

    def pair(k):
        return jnp.where(lane < CAP, ids_v[k], pltpu.roll(ids_v[k + 1], CAP, 1))

    def gather_in(g):
        wanted = jnp.concatenate([pair(4 * g), pair(4 * g + 2)], axis=1)
        values = arr_v[g % 2].reshape(4 * CAP, E)

        def block(i, carry):
            first = pl.multiple_of(i * 512, 512)
            hits = jnp.where(place512 == wanted - first, 1.0, 0.0).astype(BF)
            term = jnp.dot(hits, values, preferred_element_type=F32)
            rows = pl.ds(first, 512)
            if g == 0:
                acc[rows, :] = term
            elif g == N_ROW // 4 - 1:
                cold_b[rows, :] = (acc[rows, :] + term).astype(BF)
            else:
                acc[rows, :] += term
            return carry

        lax.fori_loop(0, ROWS_DEV // 512, block, 0)

    def groups(lo, hi, copy):
        for g in range(lo, hi):
            copy.wait()
            following = arrive(g + 1) if g + 1 < N_ROW // 4 else None
            gather_in(g)
            copy = following
        return copy

    copy = groups(0, 2, arrive(0))

    to_half.wait()

    def add_c(i, carry):
        rows = pl.ds(pl.multiple_of(i * 256, 256), 256)
        own_rows = pl.ds(pl.multiple_of(core * W_C + i * 256, 256), 256)
        half[rows, :] = (w_ref[own_rows, :].astype(F32) + part_c[rows, :].astype(F32)).astype(BF)
        return carry

    lax.fori_loop(0, W_C // 256, add_c, 0)
    to_x = []
    for k in range(1, NX):
        px = lax.rem(x + k, NX)
        to_x.append(
            remote(
                half.at[pl.ds(pl.multiple_of(px * W_X, W_X), W_X)], part_x.at[k - 1],
                rx_send.at[k - 1], rx_recv.at[k - 1], x_peer(k),
            )
        )
        to_x[-1].start()

    copy = groups(2, 6, copy)

    for c in to_x:
        c.wait()
    total = half[pl.ds(pl.multiple_of(x * W_X, W_X), W_X), :].astype(F32)
    for k in range(1, NX):
        total += part_x[k - 1].astype(F32)
    quarter[...] = total.astype(BF)
    to_y = []
    for k in range(1, NY):
        py = lax.rem(y + k, NY)
        to_y.append(
            remote(
                quarter.at[pl.ds(pl.multiple_of(py * W_Y, W_Y), W_Y)], part_y.at[k - 1],
                ry_send.at[k - 1], ry_recv.at[k - 1], y_peer(k),
            )
        )
        to_y[-1].start()

    copy = groups(6, 9, copy)

    for c in to_y:
        c.wait()
    total = quarter[pl.ds(pl.multiple_of(y * W_Y, W_Y), W_Y), :].astype(F32)
    for k in range(1, NY):
        total += part_y[k - 1].astype(F32)
    eighth[0:W_Y, :] = total
    eighth[W_Y : NZ * W_Z, :] = jnp.zeros((NZ * W_Z - W_Y, E), F32)
    to_z = []
    for k in range(1, NZ):
        pz = lax.rem(z + k, NZ)
        to_z.append(
            remote(
                eighth.at[pl.ds(pl.multiple_of(pz * W_Z, W_Z), W_Z)], part_z.at[k - 1],
                rz_send.at[k - 1], rz_recv.at[k - 1], z_peer(k),
            )
        )
        to_z[-1].start()

    groups(9, N_ROW // 4, copy)

    def g_rows(c, j):
        return pl.ds(pl.multiple_of(c * G_C + j * G_Y, G_Y), G_Y)

    to_core = []
    for k in range(1, NY + 1):
        j = lax.rem(y + k, NY)
        to_core.append(
            remote(
                cold_b.at[g_rows(1 - core, j)], got_c.at[k - 1], c_send.at[k - 1],
                c_recv.at[k - 1], sibling,
            )
        )
        to_core[-1].start()

    for c in to_z:
        c.wait()
    total = eighth[pl.ds(pl.multiple_of(z * W_Z, W_Z), W_Z), :]
    for k in range(1, NZ):
        total += part_z[k - 1]
    summed[...] = total
    gath_z[0] = total
    over_z = []
    for k in range(1, NZ):
        over_z.append(
            remote(summed, gath_z.at[k], wz_send.at[k - 1], wz_recv.at[k - 1], z_peer(k))
        )
        over_z[-1].start()

    over_y = []
    for k in range(1, NY + 1):
        j = lax.rem(y + k, NY)
        to_core[k - 1].wait_recv()
        total = cold_b[g_rows(core, j), :].astype(F32) + got_c[k - 1].astype(F32)
        if k < NY:
            mine[k - 1] = total.astype(BF)
            over_y.append(
                remote(
                    mine.at[k - 1], got_y.at[k - 1], y_send.at[k - 1], y_recv.at[k - 1], y_peer(k)
                )
            )
            over_y[-1].start()

    for c in over_z:
        c.wait()

    def place(k, carry):
        owner_z = lax.rem(z - k + NZ, NZ)
        w_y[pl.ds(pl.multiple_of(owner_z * W_Z, W_Z), W_Z), :] = gath_z[k]
        return carry

    lax.fori_loop(0, NZ, place, 0)
    gath_y[y] = w_y[0:W_Y, :].astype(BF)
    w_over_y = []
    for k in range(1, NY):
        w_over_y.append(
            remote(gath_y.at[y], gath_y.at[y], wy_send.at[k - 1], wy_recv.at[k - 1], y_peer(k))
        )
        w_over_y[-1].start()

    for k in range(1, NY):
        over_y[k - 1].wait_recv()
        total += got_y[k - 1].astype(F32)
    final[...] = total.astype(BF)
    share_y = []
    for k in range(1, NY):
        share_y.append(
            remote(
                final, cold_out.at[g_rows(core, y)], a_send.at[k - 1], a_recv.at[k - 1], y_peer(k)
            )
        )
        share_y[-1].start()
    share_c = [
        remote(final, cold_out.at[g_rows(core, y)], b_send.at[0], b_recv.at[0], sibling)
    ]
    share_c[0].start()
    cold_out[g_rows(core, y), :] = final[...]

    for c in w_over_y:
        c.wait()
    w_over_x = []
    for k in range(1, NX):
        w_over_x.append(
            remote(gath_y, gath_x.at[x], wx_send.at[k - 1], wx_recv.at[k - 1], x_peer(k))
        )
        w_over_x[-1].start()
    gath_x[x] = gath_y[...]

    for k in range(1, NY):
        share_y[k - 1].wait_recv()
        j = lax.rem(y - k + NY, NY)
        rows = cold_out.at[g_rows(core, j)]
        share_c.append(remote(rows, rows, b_send.at[k], b_recv.at[k], sibling))
        share_c[-1].start()

    for c in w_over_x:
        c.wait()
    w_over_c = remote(gath_x, w_out.at[core], wc_sem.at[0], wc_sem.at[1], sibling)
    w_over_c.start()
    w_out[core] = gath_x[...]

    for k in range(1, N_ROW):
        asks[k].wait_send()
        sends[k].wait_send()
        remote(
            stage.at[k], rows_any.at[me], row_send.at[k], row_recv.at[k], (rep, to(k))
        ).wait_send()
    for c in to_core + over_y + share_y:
        c.wait_send()
    for c in share_c:
        c.wait()
    w_over_c.wait()


def step(requests, cold_bags, hot_bags, bottom_weight, table, dense, upstream, top_weight, hot):
    dma = pltpu.SemaphoreType.DMA
    hbm = pl.BlockSpec(memory_space=pl.ANY)
    v = pltpu.VMEM
    rows = (N_ROW, CAP, E)
    return pl.pallas_call(
        step_kernel,
        out_shape=(
            jax.ShapeDtypeStruct((ROWS_DEV, E), BF),
            jax.ShapeDtypeStruct((NC, NX, NY, W_Y, E), BF),
            jax.ShapeDtypeStruct(rows, BF),
            jax.ShapeDtypeStruct(rows, BF),
        ),
        in_specs=[vmem()] * 4 + [hbm] * 5,
        out_specs=(vmem(), vmem(), hbm, hbm),
        scratch_shapes=[
            v((N_ROW, 1, 128), jnp.int32),
            v((N_ROW, 1, 128), jnp.int32),
            pltpu.SMEM((N_ROW, 1, 128), jnp.int32),
            v((ROWS_DEV, E), BF),
            v((ROWS_DEV, E), F32),
            v((CAP, E), F32),
            v(rows, BF),
            v(rows, BF),
            v((B_DEV, D_BOT), BF),
            v((B_DEV, H_TOP), BF),
            v((3 * E, H_TOP), BF),
            v((HOT, E), BF),
            v((SLOTS, B_DEV), BF),
            v((HOT, B_DEV), BF),
            v((B_DEV, 3 * E), BF),
            v((3 * E, B_DEV), BF),
            v((B_DEV, H_TOP), BF),
            v((B_DEV, 3 * E), F32),
            v(rows, BF),
            v((W_ROWS, E), BF),
            v((2, 4, CAP, E), BF),
            v((ROWS_DEV, E), F32),
            v((ROWS_DEV, E), BF),
            v((W_C, E), BF),
            v((W_C, E), BF),
            v((NX - 1, W_X, E), BF),
            v((W_X, E), BF),
            v((NY - 1, W_Y, E), BF),
            v((NZ * W_Z, E), F32),
            v((NZ - 1, W_Z, E), F32),
            v((W_Z, E), F32),
            v((NY, G_Y, E), BF),
            v((NY - 1, G_Y, E), BF),
            v((NY - 1, G_Y, E), BF),
            v((G_Y, E), BF),
            v((NZ, W_Z, E), F32),
            v((NZ * W_Z, E), F32),
            v((NY, W_Y, E), BF),
            v((NX, NY, W_Y, E), BF),
            dma((5,)),
        ]
        + [dma((N_ROW,))] * 6
        + [dma((2,)), dma((2,))]
        + [dma((NX - 1,))] * 2
        + [dma((NY - 1,))] * 2
        + [dma((NZ - 1,))] * 2
        + [dma((NY,))] * 2
        + [dma((NY - 1,))] * 4
        + [dma((NY,))] * 2
        + [dma((NZ - 1,))] * 2
        + [dma((NY - 1,))] * 2
        + [dma((NX - 1,))] * 2
        + [dma((2,))],
        compiler_params=pltpu.CompilerParams(
            collective_id=0, has_side_effects=True, vmem_limit_bytes=VMEM_LIMIT
        ),
        name="step",
    )(requests, cold_bags, hot_bags, bottom_weight, table, dense, upstream, top_weight, hot)


def widen_kernel(cold_ref, w_ref, top_out, bottom_out, hot_out, cold_out):
    for j in range(H_TOP // E):
        top_out[:, j * E : (j + 1) * E] = w_ref[j * 3 * E : (j + 1) * 3 * E, :].astype(F32)
    bottom_out[...] = w_ref[W_BOTTOM:W_HOT, :].astype(F32)
    hot_out[...] = w_ref[W_HOT:W_USED, :].astype(F32)
    cold_out[...] = cold_ref[...].astype(F32)


def widen(cold, w):
    return pl.pallas_call(
        widen_kernel,
        out_shape=(
            jax.ShapeDtypeStruct((3 * E, H_TOP), F32),
            jax.ShapeDtypeStruct((D_BOT, E), F32),
            jax.ShapeDtypeStruct((HOT, E), F32),
            jax.ShapeDtypeStruct((ROWS_DEV, E), F32),
        ),
        in_specs=[vmem()] * 2,
        out_specs=(vmem(),) * 4,
        compiler_params=pltpu.CompilerParams(vmem_limit_bytes=VMEM_LIMIT),
        name="widen",
    )(cold, w)


def local(
    dense_act,
    upstream,
    bottom_weight,
    top_weight,
    hot_table,
    cold_table,
    hot_bags,
    cold_bags,
    requests,
):
    cold, w, _, _ = step(
        requests.reshape(N_ROW, 1, CAP), cold_bags.T, hot_bags.T, bottom_weight, cold_table,
        dense_act, upstream, top_weight, hot_table,
    )
    return widen(cold, w.reshape(W_ROWS, E))


def solution(mesh):
    placed = (
        P(("rep", "row"), None),
        P(("rep", "row"), None),
        P(),
        P(),
        P(),
        P("row", None),
        P(("rep", "row"), None),
        P(("rep", "row"), None),
        P("rep", "row", None, None),
    )
    return jax.shard_map(
        local,
        mesh=mesh,
        in_specs=placed,
        out_specs=(P(), P(), P(), P("row", None)),
        check_vma=False,
    )
```

```python
import jax
import jax.numpy as jnp
from jax import lax
from jax.experimental import pallas as pl
from jax.experimental.pallas import tpu as pltpu
from jax.sharding import PartitionSpec as P

E = 128
D_BOT = 256
H_TOP = 1024
B_DEV = 512
L = 16
LH = 8
CAP = 64
ROWS_DEV = 4096
HOT = 512
N_ROW = 48
N_REP = 16
SLOTS = N_ROW * CAP
NX, NY, NZ, NC = 4, 8, 12, 2

W_BOTTOM = 3 * E * (H_TOP // E)
W_HOT = W_BOTTOM + D_BOT
W_USED = W_HOT + HOT
W_ROWS = 4096
W_C = W_ROWS // NC
W_X = W_C // NX
W_Y = W_X // NY
W_Z = 8

G_C = ROWS_DEV // NC
G_Y = G_C // NY

BF = jnp.bfloat16
F32 = jnp.float32
VMEM_LIMIT = 56 * 1024 * 1024


def vmem():
    return pl.BlockSpec(memory_space=pltpu.VMEM)


def remote(src, dst, send_sem, recv_sem, device):
    return pltpu.make_async_remote_copy(
        src_ref=src,
        dst_ref=dst,
        send_sem=send_sem,
        recv_sem=recv_sem,
        device_id=device,
        device_id_type=pl.DeviceIdType.MESH,
    )


def signal(sem, device):
    pl.semaphore_signal(sem, inc=1, device_id=device, device_id_type=pl.DeviceIdType.MESH)


def position():
    rep = lax.axis_index("rep")
    row = lax.axis_index("row")
    return rep, row


def silu_slope(value):
    sigma = jax.nn.sigmoid(value)
    return sigma * (1.0 + value * (1.0 - sigma))


def contract_first(a, b):
    return lax.dot_general(a, b, (((0,), (0,)), ((), ())), preferred_element_type=F32)


def contract_last(a, b):
    return lax.dot_general(a, b, (((1,), (1,)), ((), ())), preferred_element_type=F32)


def offset(k, core):
    dx = k % NX
    j = k // NX
    dz = (j + 1) // 2 if j % 2 else -(j // 2)
    return dx, dz * (1 - 2 * core)


def offset_of(k, core):
    dx = lax.rem(k, NX)
    j = lax.div(k, NX)
    odd = lax.rem(j, 2)
    dz = odd * lax.div(j + 1, 2) - (1 - odd) * lax.div(j, 2)
    return dx, dz * (1 - 2 * core)


def step_kernel(
    req_ref, cold_ref, hot_ref, bw_ref, table_any, dense_any, up_any, tw_any, hott_any,
    cold_out, w_out, rows_any, arr_any,
    req_pad, ids_v, ids_smem, table, table32, stage32, stage, fetched,
    dense_ref, up_ref, tw_ref, hott_ref, cold_counts, hot_counts, feats, feats_t, deltas, fgrad,
    slot, w_ref, arr_v, wanted, hits, give_c,
    part_c, half, part_x, quarter, part_y, eighth, part_z, summed,
    got_c, mine, got_y, final, gath_z, w_y, gath_y, gath_x,
    load_sem, req_send, req_recv, row_send, row_recv, arr_send, arr_recv,
    arr_sem, wc, rx_send, rx_recv, ry_send, ry_recv, rz_send, rz_recv,
    c_send, c_recv, y_send, y_recv, a_send, a_recv, b_send, b_recv,
    wz_send, wz_recv, wy_send, wy_recv, wx_send, wx_recv, wc_sem,
):
    rep, me = position()
    y, core = rep // NC, lax.rem(rep, NC)
    x, z = me // NZ, lax.rem(me, NZ)
    sibling = (y * NC + 1 - core, me)

    def to(k):
        dx, dz = offset(k, core)
        return lax.rem(x + dx, NX) * NZ + lax.rem(z + dz + NZ, NZ)

    def y_peer(k):
        return (lax.rem(y + k, NY) * NC + core, me)

    def x_peer(k):
        return (rep, lax.rem(x + k, NX) * NZ + z)

    def z_peer(k):
        return (rep, x * NZ + lax.rem(z + k, NZ))

    loads = []
    for i, (src, dst) in enumerate(
        (
            (table_any, table), (dense_any, dense_ref), (up_any, up_ref), (tw_any, tw_ref),
            (hott_any, hott_ref),
        )
    ):
        loads.append(pltpu.make_async_copy(src, dst, load_sem.at[i]))
        loads[-1].start()

    barrier = pltpu.get_barrier_semaphore()
    for k in range(1, N_ROW):
        signal(barrier, (rep, to(k)))
    signal(barrier, sibling)
    for k in range(1, NY):
        signal(barrier, y_peer(k))
    req_pad[:, :, 0:CAP] = req_ref[...]
    req_pad[:, :, CAP:128] = jnp.zeros((N_ROW, 1, 128 - CAP), jnp.int32)
    loads[0].wait()

    def widen(i, carry):
        rows = pl.ds(pl.multiple_of(i * 256, 256), 256)
        table32[rows, :] = table[rows, :].astype(F32)
        return carry

    lax.fori_loop(0, ROWS_DEV // 256, widen, 0)

    pl.semaphore_wait(barrier, N_ROW - 1 + 1 + NY - 1)

    asks = [None]
    for k in range(1, N_ROW):
        peer = to(k)
        asks.append(
            remote(req_pad.at[peer], ids_v.at[k], req_send.at[k], req_recv.at[k], (rep, peer))
        )
        asks[-1].start()
    ids_v[0] = req_pad[me]

    for k in range(1, N_ROW):
        asks[k].wait_recv()
    read = pltpu.make_async_copy(ids_v, ids_smem, load_sem.at[0])
    read.start()
    read.wait()

    def pick(k):
        for i in range(CAP):
            row = ids_smem[k, 0, i]
            stage32[pl.ds(i, 1), :] = table32[pl.ds(row, 1), :]
        stage[k] = stage32[...].astype(BF)

    def serve(k, carry):
        dx, dz = offset_of(k, core)
        peer = lax.rem(x - dx + NX, NX) * NZ + lax.rem(z - dz + NZ, NZ)
        pick(k)
        remote(
            stage.at[k], rows_any.at[me], row_send.at[k], row_recv.at[k], (rep, peer)
        ).start()
        return carry

    lax.fori_loop(1, N_ROW, serve, 0)
    pick(0)
    own = pltpu.make_async_copy(stage.at[0], rows_any.at[me], load_sem.at[0])
    own.start()

    low = lax.broadcasted_iota(jnp.int32, (128, 128), 0)

    def count(j, carry):
        lanes = pl.ds(pl.multiple_of(j * 128, 128), 128)
        ids = cold_ref[:, lanes]
        lo = ids & 127
        hi = ids >> 7
        word = (hi * 43) >> 8
        amount = jnp.left_shift(jnp.ones_like(hi), 5 * (hi - 6 * word))
        for w in range(4):
            key = jnp.where(word == w, lo, -1)
            total = jnp.zeros((128, 128), jnp.int32)
            for l in range(L):
                total += jnp.where(low == key[l : l + 1, :], amount[l : l + 1, :], 0)
            for f in range(6):
                slab = ((total >> (5 * f)) & 31).astype(F32).astype(BF)
                cold_counts[(6 * w + f) * 128 : (6 * w + f + 1) * 128, lanes] = slab
        ids = hot_ref[:, lanes]
        lo = ids & 127
        amount = jnp.left_shift(jnp.ones_like(ids), 4 * (ids >> 7))
        total = jnp.zeros((128, 128), jnp.int32)
        for l in range(LH):
            total += jnp.where(low == lo[l : l + 1, :], amount[l : l + 1, :], 0)
        for f in range(4):
            slab = ((total >> (4 * f)) & 15).astype(F32).astype(BF)
            hot_counts[f * 128 : (f + 1) * 128, lanes] = slab
        return carry

    lax.fori_loop(0, B_DEV // 128, count, 0)

    lane = lax.broadcasted_iota(jnp.int32, (1, 128), 1)
    for j in range(N_ROW // 2):
        wanted[:, 128 * j : 128 * j + 128] = jnp.where(
            lane < CAP, ids_v[2 * j], pltpu.roll(ids_v[2 * j + 1], CAP, 1)
        )
    place256 = lax.broadcasted_iota(jnp.int32, (256, 512), 0)

    def mark(i, carry):
        first = pl.multiple_of(i * 256, 256)
        for j in range(SLOTS // 512):
            cols = slice(512 * j, 512 * j + 512)
            found = jnp.where(place256 == wanted[:, cols] - first, 1.0, 0.0)
            hits[pl.ds(first, 256), cols] = found.astype(BF)
        return carry

    lax.fori_loop(0, ROWS_DEV // 256, mark, 0)

    loads[1].wait()
    bottom_pre = jnp.dot(dense_ref[...], bw_ref[...], preferred_element_type=F32)
    lower = bottom_pre * jax.nn.sigmoid(bottom_pre)
    feats[:, 0:E] = lower.astype(BF)
    slope = silu_slope(bottom_pre)
    fgrad[:, 0:E] = slope
    for i in range(2, 5):
        loads[i].wait()
    pool = contract_first(hott_ref[...], hot_counts[...])
    feats[:, 2 * E : 3 * E] = pool.T.astype(BF)

    own.wait()
    for k in range(1, N_ROW):
        owner_k = to(k)
        remote(
            stage.at[k], rows_any.at[owner_k], row_send.at[k], row_recv.at[k], (rep, owner_k)
        ).wait_recv()
    read = pltpu.make_async_copy(rows_any, fetched, load_sem.at[1])
    read.start()
    read.wait()

    pool = contract_first(fetched[...].reshape(SLOTS, E), cold_counts[...])
    feats[:, E : 2 * E] = pool.T.astype(BF)
    slope = fgrad[:, 0:E]
    for h in range(H_TOP // 256):
        cols = slice(h * 256, (h + 1) * 256)
        weight = tw_ref[:, cols]
        pre = jnp.dot(feats[...], weight, preferred_element_type=F32)
        delta = (up_ref[:, cols].astype(F32) * silu_slope(pre)).astype(BF)
        deltas[:, cols] = delta
        term = contract_last(delta, weight)
        if h == 0:
            fgrad[...] = term
        else:
            fgrad[...] += term
    cold_back = fgrad[:, E : 2 * E].astype(BF)
    for s in range(SLOTS // 512):
        total = jnp.dot(
            cold_counts[s * 512 : (s + 1) * 512, :], cold_back, preferred_element_type=F32
        )
        slot[8 * s : 8 * s + 8] = total.astype(BF).reshape(8, CAP, E)

    sends = [None]
    for k in range(1, N_ROW):
        peer = to(k)
        sends.append(
            remote(slot.at[peer], arr_any.at[k], arr_send.at[k], arr_recv.at[k], (rep, peer))
        )


    def issue(first, last):
        for k in range(first, last):
            sends[k].start()

    issue(1, 9)
    own = pltpu.make_async_copy(slot.at[me], arr_any.at[0], load_sem.at[0])
    own.start()

    feats_t[...] = feats[...].astype(F32).T.astype(BF)
    for h in range(H_TOP // 256):
        cols = slice(h * 256, (h + 1) * 256)
        top = jnp.dot(feats_t[...], deltas[:, cols], preferred_element_type=F32).astype(BF)
        w_ref[768 * h : 768 * h + 384, :] = top[:, 0:128]
        w_ref[768 * h + 384 : 768 * h + 768, :] = top[:, 128:256]
    bottom_delta = (fgrad[:, 0:E] * slope).astype(BF)
    w_ref[W_BOTTOM:W_HOT, :] = contract_first(dense_ref[...], bottom_delta).astype(BF)
    hot_back = fgrad[:, 2 * E : 3 * E].astype(BF)
    w_ref[W_HOT:W_USED, :] = jnp.dot(
        hot_counts[...], hot_back, preferred_element_type=F32
    ).astype(BF)
    w_ref[W_USED:W_ROWS, :] = jnp.zeros((W_ROWS - W_USED, E), BF)

    to_half = remote(
        w_ref.at[pl.ds(pl.multiple_of((1 - core) * W_C, W_C), W_C)], part_c, wc.at[0], wc.at[1],
        sibling,
    )
    to_half.start()
    issue(9, 15)

    to_half.wait()

    def add_c(i, carry):
        rows = pl.ds(pl.multiple_of(i * 256, 256), 256)
        own_rows = pl.ds(pl.multiple_of(core * W_C + i * 256, 256), 256)
        half[rows, :] = (w_ref[own_rows, :].astype(F32) + part_c[rows, :].astype(F32)).astype(BF)
        return carry

    lax.fori_loop(0, W_C // 256, add_c, 0)
    to_x = []
    for k in range(1, NX):
        px = lax.rem(x + k, NX)
        to_x.append(
            remote(
                half.at[pl.ds(pl.multiple_of(px * W_X, W_X), W_X)], part_x.at[k - 1],
                rx_send.at[k - 1], rx_recv.at[k - 1], x_peer(k),
            )
        )
        to_x[-1].start()
    issue(15, 21)

    for c in to_x:
        c.wait()
    total = half[pl.ds(pl.multiple_of(x * W_X, W_X), W_X), :].astype(F32)
    for k in range(1, NX):
        total += part_x[k - 1].astype(F32)
    quarter[...] = total.astype(BF)
    to_y = []
    for k in range(1, NY):
        py = lax.rem(y + k, NY)
        to_y.append(
            remote(
                quarter.at[pl.ds(pl.multiple_of(py * W_Y, W_Y), W_Y)], part_y.at[k - 1],
                ry_send.at[k - 1], ry_recv.at[k - 1], y_peer(k),
            )
        )
        to_y[-1].start()
    issue(21, 27)

    for c in to_y:
        c.wait()
    total = quarter[pl.ds(pl.multiple_of(y * W_Y, W_Y), W_Y), :].astype(F32)
    for k in range(1, NY):
        total += part_y[k - 1].astype(F32)
    eighth[0:W_Y, :] = total
    eighth[W_Y : NZ * W_Z, :] = jnp.zeros((NZ * W_Z - W_Y, E), F32)
    to_z = []
    for k in range(1, NZ):
        pz = lax.rem(z + k, NZ)
        to_z.append(
            remote(
                eighth.at[pl.ds(pl.multiple_of(pz * W_Z, W_Z), W_Z)], part_z.at[k - 1],
                rz_send.at[k - 1], rz_recv.at[k - 1], z_peer(k),
            )
        )
        to_z[-1].start()
    issue(27, 33)

    for c in to_z:
        c.wait()
    total = eighth[pl.ds(pl.multiple_of(z * W_Z, W_Z), W_Z), :]
    for k in range(1, NZ):
        total += part_z[k - 1]
    summed[...] = total
    gath_z[0] = total
    over_z = []
    for k in range(1, NZ):
        over_z.append(
            remote(summed, gath_z.at[k], wz_send.at[k - 1], wz_recv.at[k - 1], z_peer(k))
        )
        over_z[-1].start()
    issue(33, 39)

    for c in over_z:
        c.wait()

    def place(k, carry):
        owner_z = lax.rem(z - k + NZ, NZ)
        w_y[pl.ds(pl.multiple_of(owner_z * W_Z, W_Z), W_Z), :] = gath_z[k]
        return carry

    lax.fori_loop(0, NZ, place, 0)
    gath_y[y] = w_y[0:W_Y, :].astype(BF)
    w_over_y = []
    for k in range(1, NY):
        w_over_y.append(
            remote(gath_y.at[y], gath_y.at[y], wy_send.at[k - 1], wy_recv.at[k - 1], y_peer(k))
        )
        w_over_y[-1].start()
    issue(39, 44)

    for c in w_over_y:
        c.wait()
    w_over_x = []
    for k in range(1, NX):
        w_over_x.append(
            remote(gath_y, gath_x.at[x], wx_send.at[k - 1], wx_recv.at[k - 1], x_peer(k))
        )
        w_over_x[-1].start()
    issue(44, N_ROW)
    gath_x[x] = gath_y[...]

    copies = []
    for part in range(4):
        for k in range(12 * part, 12 * part + 12):
            if k == 0:
                own.wait()
            else:
                sends[k].wait_recv()
        chunk = pl.ds(12 * part, 12)
        copies.append(
            pltpu.make_async_copy(arr_any.at[chunk], arr_v.at[chunk], arr_sem.at[part])
        )
        copies[-1].start()
    for c in copies:
        c.wait()

    def g_rows(c, j):
        return pl.ds(pl.multiple_of(c * G_C + j * G_Y, G_Y), G_Y)

    sign = 1 - 2 * core

    def ring(step):
        return lax.rem(y + step + NY, NY)

    def ring_peer(step):
        return (ring(step) * NC + core, me)

    def steps(s):
        return [4, s, -s, 2 * s, -2 * s, -3 * s, 3 * s, 0]

    def owned(c, j):
        values = arr_v[...].reshape(SLOTS, E)
        total = jnp.dot(hits[g_rows(c, j), :], values, preferred_element_type=F32)
        return total.astype(BF)

    to_core = []
    for i, step in enumerate(steps(-sign)):
        give_c[i] = owned(1 - core, ring(step))
        to_core.append(
            remote(give_c.at[i], got_c.at[i], c_send.at[i], c_recv.at[i], sibling)
        )
        to_core[-1].start()

    over_y = []
    for i, step in enumerate(steps(sign)):
        total = owned(core, ring(step)).astype(F32)
        to_core[i].wait_recv()
        total += got_c[i].astype(F32)
        if i == NY - 2:
            over_y[0].wait_recv()
            total += got_y[0].astype(F32)
        if i < NY - 1:
            mine[i] = total.astype(BF)
            peer = ring_peer(sign) if i == 0 else ring_peer(step)
            over_y.append(remote(mine.at[i], got_y.at[i], y_send.at[i], y_recv.at[i], peer))
            over_y[-1].start()

    for c in w_over_x:
        c.wait()
    w_over_c = remote(gath_x, w_out.at[core], wc_sem.at[0], wc_sem.at[1], sibling)
    w_over_c.start()
    w_out[core] = gath_x[...]

    for i in range(1, NY - 1):
        over_y[i].wait_recv()
        total += got_y[i].astype(F32)
    final[...] = total.astype(BF)
    share_y = []
    for i, step in enumerate(steps(sign)[1:7]):
        share_y.append(
            remote(
                final, cold_out.at[g_rows(core, y)], a_send.at[i], a_recv.at[i], ring_peer(step)
            )
        )
        share_y[-1].start()
    share_c = [
        remote(final, cold_out.at[g_rows(core, y)], b_send.at[0], b_recv.at[0], sibling)
    ]
    share_c[0].start()
    cold_out[g_rows(core, y), :] = final[...]

    def forward(i, step):
        rows = cold_out.at[g_rows(core, ring(-step))]
        share_c.append(remote(rows, rows, b_send.at[i], b_recv.at[i], sibling))
        share_c[-1].start()

    share_y[5].wait_recv()
    rows = cold_out.at[g_rows(core, ring(-3 * sign))]
    share_y.append(remote(rows, rows, a_send.at[6], a_recv.at[6], ring_peer(sign)))
    share_y[6].start()
    forward(6, 3 * sign)
    for i, step in enumerate(steps(sign)[1:6]):
        share_y[i].wait_recv()
        forward(i + 1, step)
    share_y[6].wait_recv()
    forward(7, 4)

    for k in range(1, N_ROW):
        asks[k].wait_send()
        sends[k].wait_send()
        remote(
            stage.at[k], rows_any.at[me], row_send.at[k], row_recv.at[k], (rep, to(k))
        ).wait_send()
    for c in to_core + over_y + share_y:
        c.wait_send()
    for c in share_c:
        c.wait()
    w_over_c.wait()


def step(requests, cold_bags, hot_bags, bottom_weight, table, dense, upstream, top_weight, hot):
    dma = pltpu.SemaphoreType.DMA
    hbm = pl.BlockSpec(memory_space=pl.ANY)
    v = pltpu.VMEM
    rows = (N_ROW, CAP, E)
    return pl.pallas_call(
        step_kernel,
        out_shape=(
            jax.ShapeDtypeStruct((ROWS_DEV, E), BF),
            jax.ShapeDtypeStruct((NC, NX, NY, W_Y, E), BF),
            jax.ShapeDtypeStruct(rows, BF),
            jax.ShapeDtypeStruct(rows, BF),
        ),
        in_specs=[vmem()] * 4 + [hbm] * 5,
        out_specs=(vmem(), vmem(), hbm, hbm),
        scratch_shapes=[
            v((N_ROW, 1, 128), jnp.int32),
            v((N_ROW, 1, 128), jnp.int32),
            pltpu.SMEM((N_ROW, 1, 128), jnp.int32),
            v((ROWS_DEV, E), BF),
            v((ROWS_DEV, E), F32),
            v((CAP, E), F32),
            v(rows, BF),
            v(rows, BF),
            v((B_DEV, D_BOT), BF),
            v((B_DEV, H_TOP), BF),
            v((3 * E, H_TOP), BF),
            v((HOT, E), BF),
            v((SLOTS, B_DEV), BF),
            v((HOT, B_DEV), BF),
            v((B_DEV, 3 * E), BF),
            v((3 * E, B_DEV), BF),
            v((B_DEV, H_TOP), BF),
            v((B_DEV, 3 * E), F32),
            v(rows, BF),
            v((W_ROWS, E), BF),
            v(rows, BF),
            v((1, SLOTS), jnp.int32),
            v((ROWS_DEV, SLOTS), BF),
            v((NY, G_Y, E), BF),
            v((W_C, E), BF),
            v((W_C, E), BF),
            v((NX - 1, W_X, E), BF),
            v((W_X, E), BF),
            v((NY - 1, W_Y, E), BF),
            v((NZ * W_Z, E), F32),
            v((NZ - 1, W_Z, E), F32),
            v((W_Z, E), F32),
            v((NY, G_Y, E), BF),
            v((NY - 1, G_Y, E), BF),
            v((NY - 1, G_Y, E), BF),
            v((G_Y, E), BF),
            v((NZ, W_Z, E), F32),
            v((NZ * W_Z, E), F32),
            v((NY, W_Y, E), BF),
            v((NX, NY, W_Y, E), BF),
            dma((5,)),
        ]
        + [dma((N_ROW,))] * 6
        + [dma((4,)), dma((2,))]
        + [dma((NX - 1,))] * 2
        + [dma((NY - 1,))] * 2
        + [dma((NZ - 1,))] * 2
        + [dma((NY,))] * 2
        + [dma((NY - 1,))] * 4
        + [dma((NY,))] * 2
        + [dma((NZ - 1,))] * 2
        + [dma((NY - 1,))] * 2
        + [dma((NX - 1,))] * 2
        + [dma((2,))],
        compiler_params=pltpu.CompilerParams(
            collective_id=0, has_side_effects=True, vmem_limit_bytes=VMEM_LIMIT
        ),
        name="step",
    )(requests, cold_bags, hot_bags, bottom_weight, table, dense, upstream, top_weight, hot)


def widen_kernel(cold_ref, w_ref, top_out, bottom_out, hot_out, cold_out):
    for j in range(H_TOP // E):
        top_out[:, j * E : (j + 1) * E] = w_ref[j * 3 * E : (j + 1) * 3 * E, :].astype(F32)
    bottom_out[...] = w_ref[W_BOTTOM:W_HOT, :].astype(F32)
    hot_out[...] = w_ref[W_HOT:W_USED, :].astype(F32)
    cold_out[...] = cold_ref[...].astype(F32)


def widen(cold, w):
    return pl.pallas_call(
        widen_kernel,
        out_shape=(
            jax.ShapeDtypeStruct((3 * E, H_TOP), F32),
            jax.ShapeDtypeStruct((D_BOT, E), F32),
            jax.ShapeDtypeStruct((HOT, E), F32),
            jax.ShapeDtypeStruct((ROWS_DEV, E), F32),
        ),
        in_specs=[vmem()] * 2,
        out_specs=(vmem(),) * 4,
        compiler_params=pltpu.CompilerParams(vmem_limit_bytes=VMEM_LIMIT),
        name="widen",
    )(cold, w)


def local(
    dense_act,
    upstream,
    bottom_weight,
    top_weight,
    hot_table,
    cold_table,
    hot_bags,
    cold_bags,
    requests,
):
    cold, w, _, _ = step(
        requests.reshape(N_ROW, 1, CAP), cold_bags.T, hot_bags.T, bottom_weight, cold_table,
        dense_act, upstream, top_weight, hot_table,
    )
    return widen(cold, w.reshape(W_ROWS, E))


def solution(mesh):
    placed = (
        P(("rep", "row"), None),
        P(("rep", "row"), None),
        P(),
        P(),
        P(),
        P("row", None),
        P(("rep", "row"), None),
        P(("rep", "row"), None),
        P("rep", "row", None, None),
    )
    return jax.shard_map(
        local,
        mesh=mesh,
        in_specs=placed,
        out_specs=(P(), P(), P(), P("row", None)),
        check_vma=False,
    )
```

```python
import jax
import jax.numpy as jnp
from jax import lax
from jax.experimental import pallas as pl
from jax.experimental.pallas import tpu as pltpu
from jax.sharding import PartitionSpec as P

E = 128
D_BOT = 256
H_TOP = 1024
B_DEV = 512
L = 16
LH = 8
CAP = 64
ROWS_DEV = 4096
HOT = 512
N_ROW = 48
N_REP = 16
SLOTS = N_ROW * CAP
NX, NY, NZ, NC = 4, 8, 12, 2

W_BOTTOM = 3 * E * (H_TOP // E)
W_HOT = W_BOTTOM + D_BOT
W_USED = W_HOT + HOT
W_ROWS = 4096
W_C = W_ROWS // NC
W_Y = W_C // NY
W_X = W_Y // NX
W_Z = 8

G_C = ROWS_DEV // NC
G_Y = G_C // NY

BF = jnp.bfloat16
F32 = jnp.float32
VMEM_LIMIT = 56 * 1024 * 1024


def vmem():
    return pl.BlockSpec(memory_space=pltpu.VMEM)


def remote(src, dst, send_sem, recv_sem, device):
    return pltpu.make_async_remote_copy(
        src_ref=src,
        dst_ref=dst,
        send_sem=send_sem,
        recv_sem=recv_sem,
        device_id=device,
        device_id_type=pl.DeviceIdType.MESH,
    )


def signal(sem, device):
    pl.semaphore_signal(sem, inc=1, device_id=device, device_id_type=pl.DeviceIdType.MESH)


def position():
    rep = lax.axis_index("rep")
    row = lax.axis_index("row")
    return rep, row


def silu_slope(value):
    sigma = jax.nn.sigmoid(value)
    return sigma * (1.0 + value * (1.0 - sigma))


def contract_first(a, b):
    return lax.dot_general(a, b, (((0,), (0,)), ((), ())), preferred_element_type=F32)


def contract_last(a, b):
    return lax.dot_general(a, b, (((1,), (1,)), ((), ())), preferred_element_type=F32)


def offset(k, core):
    dx = k % NX
    j = k // NX
    dz = (j + 1) // 2 if j % 2 else -(j // 2)
    return dx, dz * (1 - 2 * core)


def offset_of(k, core):
    dx = lax.rem(k, NX)
    j = lax.div(k, NX)
    odd = lax.rem(j, 2)
    dz = odd * lax.div(j + 1, 2) - (1 - odd) * lax.div(j, 2)
    return dx, dz * (1 - 2 * core)


def step_kernel(
    req_ref, cold_ref, hot_ref, bw_ref, table_any, dense_any, up_any, tw_any, hott_any,
    cold_out, w_out, rows_any, arr_any,
    req_pad, ids_v, ids_smem, table, table32, stage32, stage, fetched,
    dense_ref, up_ref, tw_ref, hott_ref, cold_counts, hot_counts, feats, feats_t, deltas, fgrad,
    slot, w_ref, arr_v, wanted, hits, give_c,
    part_c, half, part_x, quarter, part_y, eighth, part_z, summed,
    got_c, mine, got_y, final, gath_z, w_x, gath_x, gath_y,
    load_sem, req_send, req_recv, row_send, row_recv, arr_send, arr_recv,
    arr_sem, wc, rx_send, rx_recv, ry_send, ry_recv, rz_send, rz_recv,
    c_send, c_recv, y_send, y_recv, a_send, a_recv, b_send, b_recv,
    wz_send, wz_recv, wy_send, wy_recv, wx_send, wx_recv, wc_sem,
):
    rep, me = position()
    y, core = rep // NC, lax.rem(rep, NC)
    x, z = me // NZ, lax.rem(me, NZ)
    sibling = (y * NC + 1 - core, me)

    def to(k):
        dx, dz = offset(k, core)
        return lax.rem(x + dx, NX) * NZ + lax.rem(z + dz + NZ, NZ)

    def y_peer(k):
        return (lax.rem(y + k, NY) * NC + core, me)

    def x_peer(k):
        return (rep, lax.rem(x + k, NX) * NZ + z)

    def z_peer(k):
        return (rep, x * NZ + lax.rem(z + k, NZ))

    loads = []
    for i, (src, dst) in enumerate(
        (
            (table_any, table), (dense_any, dense_ref), (up_any, up_ref), (tw_any, tw_ref),
            (hott_any, hott_ref),
        )
    ):
        loads.append(pltpu.make_async_copy(src, dst, load_sem.at[i]))
        loads[-1].start()

    barrier = pltpu.get_barrier_semaphore()
    for k in range(1, N_ROW):
        signal(barrier, (rep, to(k)))
    signal(barrier, sibling)
    for k in range(1, NY):
        signal(barrier, y_peer(k))
    req_pad[:, :, 0:CAP] = req_ref[...]
    req_pad[:, :, CAP:128] = jnp.zeros((N_ROW, 1, 128 - CAP), jnp.int32)
    loads[0].wait()

    def widen(i, carry):
        rows = pl.ds(pl.multiple_of(i * 256, 256), 256)
        table32[rows, :] = table[rows, :].astype(F32)
        return carry

    lax.fori_loop(0, ROWS_DEV // 256, widen, 0)

    pl.semaphore_wait(barrier, N_ROW - 1 + 1 + NY - 1)

    asks = [None]
    for k in range(1, N_ROW):
        peer = to(k)
        asks.append(
            remote(req_pad.at[peer], ids_v.at[k], req_send.at[k], req_recv.at[k], (rep, peer))
        )
        asks[-1].start()
    ids_v[0] = req_pad[me]

    for k in range(1, N_ROW):
        asks[k].wait_recv()
    read = pltpu.make_async_copy(ids_v, ids_smem, load_sem.at[0])
    read.start()
    read.wait()

    def pick(k):
        for i in range(CAP):
            row = ids_smem[k, 0, i]
            stage32[pl.ds(i, 1), :] = table32[pl.ds(row, 1), :]
        stage[k] = stage32[...].astype(BF)

    def serve(k, carry):
        dx, dz = offset_of(k, core)
        peer = lax.rem(x - dx + NX, NX) * NZ + lax.rem(z - dz + NZ, NZ)
        pick(k)
        remote(
            stage.at[k], rows_any.at[me], row_send.at[k], row_recv.at[k], (rep, peer)
        ).start()
        return carry

    lax.fori_loop(1, N_ROW, serve, 0)
    pick(0)
    own = pltpu.make_async_copy(stage.at[0], rows_any.at[me], load_sem.at[0])
    own.start()

    low = lax.broadcasted_iota(jnp.int32, (128, 128), 0)

    def count(j, carry):
        lanes = pl.ds(pl.multiple_of(j * 128, 128), 128)
        ids = cold_ref[:, lanes]
        lo = ids & 127
        hi = ids >> 7
        word = (hi * 43) >> 8
        amount = jnp.left_shift(jnp.ones_like(hi), 5 * (hi - 6 * word))
        for w in range(4):
            key = jnp.where(word == w, lo, -1)
            total = jnp.zeros((128, 128), jnp.int32)
            for l in range(L):
                total += jnp.where(low == key[l : l + 1, :], amount[l : l + 1, :], 0)
            for f in range(6):
                slab = ((total >> (5 * f)) & 31).astype(F32).astype(BF)
                cold_counts[(6 * w + f) * 128 : (6 * w + f + 1) * 128, lanes] = slab
        ids = hot_ref[:, lanes]
        lo = ids & 127
        amount = jnp.left_shift(jnp.ones_like(ids), 4 * (ids >> 7))
        total = jnp.zeros((128, 128), jnp.int32)
        for l in range(LH):
            total += jnp.where(low == lo[l : l + 1, :], amount[l : l + 1, :], 0)
        for f in range(4):
            slab = ((total >> (4 * f)) & 15).astype(F32).astype(BF)
            hot_counts[f * 128 : (f + 1) * 128, lanes] = slab
        return carry

    lax.fori_loop(0, B_DEV // 128, count, 0)

    lane = lax.broadcasted_iota(jnp.int32, (1, 128), 1)
    for j in range(N_ROW // 2):
        wanted[:, 128 * j : 128 * j + 128] = jnp.where(
            lane < CAP, ids_v[2 * j], pltpu.roll(ids_v[2 * j + 1], CAP, 1)
        )
    place256 = lax.broadcasted_iota(jnp.int32, (256, 512), 0)

    def mark(i, carry):
        first = pl.multiple_of(i * 256, 256)
        for j in range(SLOTS // 512):
            cols = slice(512 * j, 512 * j + 512)
            found = jnp.where(place256 == wanted[:, cols] - first, 1.0, 0.0)
            hits[pl.ds(first, 256), cols] = found.astype(BF)
        return carry

    lax.fori_loop(0, ROWS_DEV // 256, mark, 0)

    loads[1].wait()
    bottom_pre = jnp.dot(dense_ref[...], bw_ref[...], preferred_element_type=F32)
    lower = bottom_pre * jax.nn.sigmoid(bottom_pre)
    feats[:, 0:E] = lower.astype(BF)
    slope = silu_slope(bottom_pre)
    fgrad[:, 0:E] = slope
    for i in range(2, 5):
        loads[i].wait()
    pool = contract_first(hott_ref[...], hot_counts[...])
    feats[:, 2 * E : 3 * E] = pool.T.astype(BF)

    own.wait()
    for k in range(1, N_ROW):
        owner_k = to(k)
        remote(
            stage.at[k], rows_any.at[owner_k], row_send.at[k], row_recv.at[k], (rep, owner_k)
        ).wait_recv()
    read = pltpu.make_async_copy(rows_any, fetched, load_sem.at[1])
    read.start()
    read.wait()

    pool = contract_first(fetched[...].reshape(SLOTS, E), cold_counts[...])
    feats[:, E : 2 * E] = pool.T.astype(BF)
    slope = fgrad[:, 0:E]
    for h in range(H_TOP // 256):
        cols = slice(h * 256, (h + 1) * 256)
        weight = tw_ref[:, cols]
        pre = jnp.dot(feats[...], weight, preferred_element_type=F32)
        delta = (up_ref[:, cols].astype(F32) * silu_slope(pre)).astype(BF)
        deltas[:, cols] = delta
        term = contract_last(delta, weight)
        if h == 0:
            fgrad[...] = term
        else:
            fgrad[...] += term
    cold_back = fgrad[:, E : 2 * E].astype(BF)
    for s in range(SLOTS // 512):
        total = jnp.dot(
            cold_counts[s * 512 : (s + 1) * 512, :], cold_back, preferred_element_type=F32
        )
        slot[8 * s : 8 * s + 8] = total.astype(BF).reshape(8, CAP, E)

    feats_t[...] = feats[...].astype(F32).T.astype(BF)
    for h in range(H_TOP // 256):
        cols = slice(h * 256, (h + 1) * 256)
        top = jnp.dot(feats_t[...], deltas[:, cols], preferred_element_type=F32).astype(BF)
        w_ref[768 * h : 768 * h + 384, :] = top[:, 0:128]
        w_ref[768 * h + 384 : 768 * h + 768, :] = top[:, 128:256]
    bottom_delta = (fgrad[:, 0:E] * slope).astype(BF)
    w_ref[W_BOTTOM:W_HOT, :] = contract_first(dense_ref[...], bottom_delta).astype(BF)
    hot_back = fgrad[:, 2 * E : 3 * E].astype(BF)
    w_ref[W_HOT:W_USED, :] = jnp.dot(
        hot_counts[...], hot_back, preferred_element_type=F32
    ).astype(BF)
    w_ref[W_USED:W_ROWS, :] = jnp.zeros((W_ROWS - W_USED, E), BF)

    to_half = remote(
        w_ref.at[pl.ds(pl.multiple_of((1 - core) * W_C, W_C), W_C)], part_c, wc.at[0], wc.at[1],
        sibling,
    )
    to_half.start()

    sends = [None]
    for k in range(1, N_ROW):
        peer = to(k)
        sends.append(
            remote(slot.at[peer], arr_any.at[k], arr_send.at[k], arr_recv.at[k], (rep, peer))
        )

        sends[-1].start()
    own = pltpu.make_async_copy(slot.at[me], arr_any.at[0], load_sem.at[0])
    own.start()

    to_half.wait()

    def add_c(i, carry):
        rows = pl.ds(pl.multiple_of(i * 256, 256), 256)
        own_rows = pl.ds(pl.multiple_of(core * W_C + i * 256, 256), 256)
        half[rows, :] = (w_ref[own_rows, :].astype(F32) + part_c[rows, :].astype(F32)).astype(BF)
        return carry

    lax.fori_loop(0, W_C // 256, add_c, 0)
    to_y = []
    for k in range(1, NY):
        py = lax.rem(y + k, NY)
        to_y.append(
            remote(
                half.at[pl.ds(pl.multiple_of(py * W_Y, W_Y), W_Y)], part_y.at[k - 1],
                ry_send.at[k - 1], ry_recv.at[k - 1], y_peer(k),
            )
        )
        to_y[-1].start()
    for c in to_y:
        c.wait()
    total = half[pl.ds(pl.multiple_of(y * W_Y, W_Y), W_Y), :].astype(F32)
    for k in range(1, NY):
        total += part_y[k - 1].astype(F32)
    quarter[...] = total.astype(BF)
    to_x = []
    for k in range(1, NX):
        px = lax.rem(x + k, NX)
        to_x.append(
            remote(
                quarter.at[pl.ds(pl.multiple_of(px * W_X, W_X), W_X)], part_x.at[k - 1],
                rx_send.at[k - 1], rx_recv.at[k - 1], x_peer(k),
            )
        )
        to_x[-1].start()

    copies = []
    for part in range(4):
        for k in range(12 * part, 12 * part + 12):
            if k == 0:
                own.wait()
            else:
                sends[k].wait_recv()
        chunk = pl.ds(12 * part, 12)
        copies.append(
            pltpu.make_async_copy(arr_any.at[chunk], arr_v.at[chunk], arr_sem.at[part])
        )
        copies[-1].start()
    for c in copies:
        c.wait()

    def g_rows(c, j):
        return pl.ds(pl.multiple_of(c * G_C + j * G_Y, G_Y), G_Y)

    sign = 1 - 2 * core

    def ring(step):
        return lax.rem(y + step + NY, NY)

    def ring_peer(step):
        return (ring(step) * NC + core, me)

    def steps(s):
        return [4, s, -s, 2 * s, -2 * s, -3 * s, 3 * s, 0]

    def owned(c, j):
        values = arr_v[...].reshape(SLOTS, E)
        total = jnp.dot(hits[g_rows(c, j), :], values, preferred_element_type=F32)
        return total.astype(BF)

    def add_x():
        for c in to_x:
            c.wait()
        total = quarter[pl.ds(pl.multiple_of(x * W_X, W_X), W_X), :].astype(F32)
        for k in range(1, NX):
            total += part_x[k - 1].astype(F32)
        eighth[0:W_X, :] = total
        eighth[W_X : NZ * W_Z, :] = jnp.zeros((NZ * W_Z - W_X, E), F32)
        copies = []
        for k in range(1, NZ):
            pz = lax.rem(z + k, NZ)
            copies.append(
                remote(
                    eighth.at[pl.ds(pl.multiple_of(pz * W_Z, W_Z), W_Z)], part_z.at[k - 1],
                    rz_send.at[k - 1], rz_recv.at[k - 1], z_peer(k),
                )
            )
            copies[-1].start()
        return copies

    def add_z():
        for c in to_z:
            c.wait()
        total = eighth[pl.ds(pl.multiple_of(z * W_Z, W_Z), W_Z), :]
        for k in range(1, NZ):
            total += part_z[k - 1]
        summed[...] = total
        gath_z[0] = total
        copies = []
        for k in range(1, NZ):
            copies.append(
                remote(summed, gath_z.at[k], wz_send.at[k - 1], wz_recv.at[k - 1], z_peer(k))
            )
            copies[-1].start()
        return copies

    to_z = add_x()
    to_core = []
    for i, step in enumerate(steps(-sign)):
        give_c[i] = owned(1 - core, ring(step))
        to_core.append(
            remote(give_c.at[i], got_c.at[i], c_send.at[i], c_recv.at[i], sibling)
        )
        to_core[-1].start()
    over_z = add_z()

    over_y = []
    for i, step in enumerate(steps(sign)):
        total = owned(core, ring(step)).astype(F32)
        to_core[i].wait_recv()
        total += got_c[i].astype(F32)
        if i == NY - 2:
            over_y[0].wait_recv()
            total += got_y[0].astype(F32)
        if i < NY - 1:
            mine[i] = total.astype(BF)
            peer = ring_peer(sign) if i == 0 else ring_peer(step)
            over_y.append(remote(mine.at[i], got_y.at[i], y_send.at[i], y_recv.at[i], peer))
            over_y[-1].start()

    for c in over_z:
        c.wait()

    def place(k, carry):
        owner_z = lax.rem(z - k + NZ, NZ)
        w_x[pl.ds(pl.multiple_of(owner_z * W_Z, W_Z), W_Z), :] = gath_z[k]
        return carry

    lax.fori_loop(0, NZ, place, 0)
    gath_y[y] = w_x[0:W_X, :].astype(BF)
    w_over_y = []
    for k in range(1, NY):
        w_over_y.append(
            remote(gath_y.at[y], gath_y.at[y], wy_send.at[k - 1], wy_recv.at[k - 1], y_peer(k))
        )
        w_over_y[-1].start()

    for i in range(1, NY - 1):
        over_y[i].wait_recv()
        total += got_y[i].astype(F32)
    final[...] = total.astype(BF)
    share_y = []
    for i, step in enumerate(steps(sign)[1:7]):
        share_y.append(
            remote(
                final, cold_out.at[g_rows(core, y)], a_send.at[i], a_recv.at[i], ring_peer(step)
            )
        )
        share_y[-1].start()
    share_c = [
        remote(final, cold_out.at[g_rows(core, y)], b_send.at[0], b_recv.at[0], sibling)
    ]
    share_c[0].start()
    cold_out[g_rows(core, y), :] = final[...]

    def forward(i, step):
        rows = cold_out.at[g_rows(core, ring(-step))]
        share_c.append(remote(rows, rows, b_send.at[i], b_recv.at[i], sibling))
        share_c[-1].start()

    for c in w_over_y:
        c.wait()
    w_over_x = []
    for k in range(1, NX):
        w_over_x.append(
            remote(gath_y, gath_x.at[x], wx_send.at[k - 1], wx_recv.at[k - 1], x_peer(k))
        )
        w_over_x[-1].start()
    gath_x[x] = gath_y[...]

    share_y[5].wait_recv()
    rows = cold_out.at[g_rows(core, ring(-3 * sign))]
    share_y.append(remote(rows, rows, a_send.at[6], a_recv.at[6], ring_peer(sign)))
    share_y[6].start()
    forward(6, 3 * sign)
    for i, step in enumerate(steps(sign)[1:6]):
        share_y[i].wait_recv()
        forward(i + 1, step)
    for c in w_over_x:
        c.wait()
    w_over_c = remote(gath_x, w_out.at[core], wc_sem.at[0], wc_sem.at[1], sibling)
    w_over_c.start()
    w_out[core] = gath_x[...]
    share_y[6].wait_recv()
    forward(7, 4)

    for k in range(1, N_ROW):
        asks[k].wait_send()
        sends[k].wait_send()
        remote(
            stage.at[k], rows_any.at[me], row_send.at[k], row_recv.at[k], (rep, to(k))
        ).wait_send()
    for c in to_core + over_y + share_y:
        c.wait_send()
    for c in share_c:
        c.wait()
    w_over_c.wait()


def step(requests, cold_bags, hot_bags, bottom_weight, table, dense, upstream, top_weight, hot):
    dma = pltpu.SemaphoreType.DMA
    hbm = pl.BlockSpec(memory_space=pl.ANY)
    v = pltpu.VMEM
    rows = (N_ROW, CAP, E)
    return pl.pallas_call(
        step_kernel,
        out_shape=(
            jax.ShapeDtypeStruct((ROWS_DEV, E), BF),
            jax.ShapeDtypeStruct((NC, NX, NY, W_X, E), BF),
            jax.ShapeDtypeStruct(rows, BF),
            jax.ShapeDtypeStruct(rows, BF),
        ),
        in_specs=[vmem()] * 4 + [hbm] * 5,
        out_specs=(vmem(), vmem(), hbm, hbm),
        scratch_shapes=[
            v((N_ROW, 1, 128), jnp.int32),
            v((N_ROW, 1, 128), jnp.int32),
            pltpu.SMEM((N_ROW, 1, 128), jnp.int32),
            v((ROWS_DEV, E), BF),
            v((ROWS_DEV, E), F32),
            v((CAP, E), F32),
            v(rows, BF),
            v(rows, BF),
            v((B_DEV, D_BOT), BF),
            v((B_DEV, H_TOP), BF),
            v((3 * E, H_TOP), BF),
            v((HOT, E), BF),
            v((SLOTS, B_DEV), BF),
            v((HOT, B_DEV), BF),
            v((B_DEV, 3 * E), BF),
            v((3 * E, B_DEV), BF),
            v((B_DEV, H_TOP), BF),
            v((B_DEV, 3 * E), F32),
            v(rows, BF),
            v((W_ROWS, E), BF),
            v(rows, BF),
            v((1, SLOTS), jnp.int32),
            v((ROWS_DEV, SLOTS), BF),
            v((NY, G_Y, E), BF),
            v((W_C, E), BF),
            v((W_C, E), BF),
            v((NX - 1, W_X, E), BF),
            v((W_Y, E), BF),
            v((NY - 1, W_Y, E), BF),
            v((NZ * W_Z, E), F32),
            v((NZ - 1, W_Z, E), F32),
            v((W_Z, E), F32),
            v((NY, G_Y, E), BF),
            v((NY - 1, G_Y, E), BF),
            v((NY - 1, G_Y, E), BF),
            v((G_Y, E), BF),
            v((NZ, W_Z, E), F32),
            v((NZ * W_Z, E), F32),
            v((NX, NY, W_X, E), BF),
            v((NY, W_X, E), BF),
            dma((5,)),
        ]
        + [dma((N_ROW,))] * 6
        + [dma((4,)), dma((2,))]
        + [dma((NX - 1,))] * 2
        + [dma((NY - 1,))] * 2
        + [dma((NZ - 1,))] * 2
        + [dma((NY,))] * 2
        + [dma((NY - 1,))] * 4
        + [dma((NY,))] * 2
        + [dma((NZ - 1,))] * 2
        + [dma((NY - 1,))] * 2
        + [dma((NX - 1,))] * 2
        + [dma((2,))],
        compiler_params=pltpu.CompilerParams(
            collective_id=0, has_side_effects=True, vmem_limit_bytes=VMEM_LIMIT
        ),
        name="step",
    )(requests, cold_bags, hot_bags, bottom_weight, table, dense, upstream, top_weight, hot)


def widen_kernel(cold_ref, w_ref, top_out, bottom_out, hot_out, cold_out):
    for c in range(NC):
        for yy in range(NY):
            for xx in range(NX):
                row = c * W_C + yy * W_Y + xx * W_X
                values = w_ref[c, xx, yy].astype(F32)
                if row < W_BOTTOM:
                    col, first = row // (3 * E), row % (3 * E)
                    top_out[first : first + W_X, col * E : (col + 1) * E] = values
                elif row < W_HOT:
                    bottom_out[row - W_BOTTOM : row - W_BOTTOM + W_X, :] = values
                elif row < W_USED:
                    hot_out[row - W_HOT : row - W_HOT + W_X, :] = values
    cold_out[...] = cold_ref[...].astype(F32)


def widen(cold, w):
    return pl.pallas_call(
        widen_kernel,
        out_shape=(
            jax.ShapeDtypeStruct((3 * E, H_TOP), F32),
            jax.ShapeDtypeStruct((D_BOT, E), F32),
            jax.ShapeDtypeStruct((HOT, E), F32),
            jax.ShapeDtypeStruct((ROWS_DEV, E), F32),
        ),
        in_specs=[vmem()] * 2,
        out_specs=(vmem(),) * 4,
        compiler_params=pltpu.CompilerParams(vmem_limit_bytes=VMEM_LIMIT),
        name="widen",
    )(cold, w)


def local(
    dense_act,
    upstream,
    bottom_weight,
    top_weight,
    hot_table,
    cold_table,
    hot_bags,
    cold_bags,
    requests,
):
    cold, w, _, _ = step(
        requests.reshape(N_ROW, 1, CAP), cold_bags.T, hot_bags.T, bottom_weight, cold_table,
        dense_act, upstream, top_weight, hot_table,
    )
    return widen(cold, w)


def solution(mesh):
    placed = (
        P(("rep", "row"), None),
        P(("rep", "row"), None),
        P(),
        P(),
        P(),
        P("row", None),
        P(("rep", "row"), None),
        P(("rep", "row"), None),
        P("rep", "row", None, None),
    )
    return jax.shard_map(
        local,
        mesh=mesh,
        in_specs=placed,
        out_specs=(P(), P(), P(), P("row", None)),
        check_vma=False,
    )
```

```python
import jax
import jax.numpy as jnp
from jax import lax
from jax.experimental import pallas as pl
from jax.experimental.pallas import tpu as pltpu
from jax.sharding import PartitionSpec as P

E = 128
D_BOT = 256
H_TOP = 1024
B_DEV = 512
L = 16
LH = 8
CAP = 64
ROWS_DEV = 4096
HOT = 512
N_ROW = 48
N_REP = 16
SLOTS = N_ROW * CAP
NX, NY, NZ, NC = 4, 8, 12, 2

W_BOTTOM = 3 * E * (H_TOP // E)
W_HOT = W_BOTTOM + D_BOT
W_USED = W_HOT + HOT
W_ROWS = 4096
W_C = W_ROWS // NC
W_Y = W_C // NY
W_X = W_Y // NX
W_Z = 8

G_C = ROWS_DEV // NC
G_Y = G_C // NY

BF = jnp.bfloat16
F32 = jnp.float32
VMEM_LIMIT = 56 * 1024 * 1024


def vmem():
    return pl.BlockSpec(memory_space=pltpu.VMEM)


def remote(src, dst, send_sem, recv_sem, device):
    return pltpu.make_async_remote_copy(
        src_ref=src,
        dst_ref=dst,
        send_sem=send_sem,
        recv_sem=recv_sem,
        device_id=device,
        device_id_type=pl.DeviceIdType.MESH,
    )


def signal(sem, device):
    pl.semaphore_signal(sem, inc=1, device_id=device, device_id_type=pl.DeviceIdType.MESH)


def position():
    rep = lax.axis_index("rep")
    row = lax.axis_index("row")
    return rep, row


def silu_slope(value):
    sigma = jax.nn.sigmoid(value)
    return sigma * (1.0 + value * (1.0 - sigma))


def contract_first(a, b):
    return lax.dot_general(a, b, (((0,), (0,)), ((), ())), preferred_element_type=F32)


def contract_last(a, b):
    return lax.dot_general(a, b, (((1,), (1,)), ((), ())), preferred_element_type=F32)


def offset(k, core):
    dx = k % NX
    j = k // NX
    dz = (j + 1) // 2 if j % 2 else -(j // 2)
    return dx, dz * (1 - 2 * core)


def offset_of(k, core):
    dx = lax.rem(k, NX)
    j = lax.div(k, NX)
    odd = lax.rem(j, 2)
    dz = odd * lax.div(j + 1, 2) - (1 - odd) * lax.div(j, 2)
    return dx, dz * (1 - 2 * core)


def step_kernel(
    req_ref, cold_ref, hot_ref, bw_ref, table_any, dense_any, up_any, tw_any, hott_any,
    cold_out, w_out, rows_any, arr_any,
    req_pad, ids_v, ids_smem, table, table32, stage32, stage, fetched,
    dense_ref, up_ref, tw_ref, hott_ref, cold_counts, hot_counts, feats, feats_t, deltas, fgrad,
    slot, w_ref, arr_v, wanted, hits, give_c,
    part_c, half, part_x, quarter, part_y, eighth, part_z, summed,
    got_c, mine, got_y, final, gath_z, w_x, gath_x, gath_y,
    load_sem, req_send, req_recv, row_send, row_recv, arr_send, arr_recv,
    arr_sem, wc, rx_send, rx_recv, ry_send, ry_recv, rz_send, rz_recv,
    c_send, c_recv, y_send, y_recv, a_send, a_recv, b_send, b_recv,
    wz_send, wz_recv, wy_send, wy_recv, wx_send, wx_recv, wc_sem,
):
    rep, me = position()
    y, core = rep // NC, lax.rem(rep, NC)
    x, z = me // NZ, lax.rem(me, NZ)
    sibling = (y * NC + 1 - core, me)

    def to(k):
        dx, dz = offset(k, core)
        return lax.rem(x + dx, NX) * NZ + lax.rem(z + dz + NZ, NZ)

    def y_peer(k):
        return (lax.rem(y + k, NY) * NC + core, me)

    def x_peer(k):
        return (rep, lax.rem(x + k, NX) * NZ + z)

    def z_peer(k):
        return (rep, x * NZ + lax.rem(z + k, NZ))

    loads = []
    for i, (src, dst) in enumerate(
        (
            (table_any, table), (dense_any, dense_ref), (up_any, up_ref), (tw_any, tw_ref),
            (hott_any, hott_ref),
        )
    ):
        loads.append(pltpu.make_async_copy(src, dst, load_sem.at[i]))
        loads[-1].start()

    barrier = pltpu.get_barrier_semaphore()
    for k in range(1, N_ROW):
        signal(barrier, (rep, to(k)))
    signal(barrier, sibling)
    for k in range(1, NY):
        signal(barrier, y_peer(k))
    req_pad[:, :, 0:CAP] = req_ref[...]
    req_pad[:, :, CAP:128] = jnp.zeros((N_ROW, 1, 128 - CAP), jnp.int32)
    loads[0].wait()

    def widen(i, carry):
        rows = pl.ds(pl.multiple_of(i * 256, 256), 256)
        table32[rows, :] = table[rows, :].astype(F32)
        return carry

    lax.fori_loop(0, ROWS_DEV // 256, widen, 0)

    pl.semaphore_wait(barrier, N_ROW - 1 + 1 + NY - 1)

    asks = [None]
    for k in range(1, N_ROW):
        peer = to(k)
        asks.append(
            remote(req_pad.at[peer], ids_v.at[k], req_send.at[k], req_recv.at[k], (rep, peer))
        )
        asks[-1].start()
    ids_v[0] = req_pad[me]

    for k in range(1, N_ROW):
        asks[k].wait_recv()
    read = pltpu.make_async_copy(ids_v, ids_smem, load_sem.at[0])
    read.start()
    read.wait()

    def pick(k):
        for i in range(CAP):
            row = ids_smem[k, 0, i]
            stage32[pl.ds(i, 1), :] = table32[pl.ds(row, 1), :]
        stage[k] = stage32[...].astype(BF)

    def serve(i, carry):
        k = N_ROW - i
        dx, dz = offset_of(k, core)
        peer = lax.rem(x - dx + NX, NX) * NZ + lax.rem(z - dz + NZ, NZ)
        pick(k)
        remote(
            stage.at[k], rows_any.at[me], row_send.at[k], row_recv.at[k], (rep, peer)
        ).start()
        return carry

    lax.fori_loop(1, N_ROW, serve, 0)
    pick(0)
    own = pltpu.make_async_copy(stage.at[0], rows_any.at[me], load_sem.at[0])
    own.start()

    low = lax.broadcasted_iota(jnp.int32, (128, 128), 0)

    def count(j, carry):
        lanes = pl.ds(pl.multiple_of(j * 128, 128), 128)
        ids = cold_ref[:, lanes]
        lo = ids & 127
        hi = ids >> 7
        word = (hi * 43) >> 8
        amount = jnp.left_shift(jnp.ones_like(hi), 5 * (hi - 6 * word))
        for w in range(4):
            key = jnp.where(word == w, lo, -1)
            total = jnp.zeros((128, 128), jnp.int32)
            for l in range(L):
                total += jnp.where(low == key[l : l + 1, :], amount[l : l + 1, :], 0)
            for f in range(6):
                slab = ((total >> (5 * f)) & 31).astype(F32).astype(BF)
                cold_counts[(6 * w + f) * 128 : (6 * w + f + 1) * 128, lanes] = slab
        ids = hot_ref[:, lanes]
        lo = ids & 127
        amount = jnp.left_shift(jnp.ones_like(ids), 4 * (ids >> 7))
        total = jnp.zeros((128, 128), jnp.int32)
        for l in range(LH):
            total += jnp.where(low == lo[l : l + 1, :], amount[l : l + 1, :], 0)
        for f in range(4):
            slab = ((total >> (4 * f)) & 15).astype(F32).astype(BF)
            hot_counts[f * 128 : (f + 1) * 128, lanes] = slab
        return carry

    lax.fori_loop(0, B_DEV // 128, count, 0)

    lane = lax.broadcasted_iota(jnp.int32, (1, 128), 1)
    for j in range(N_ROW // 2):
        wanted[:, 128 * j : 128 * j + 128] = jnp.where(
            lane < CAP, ids_v[2 * j], pltpu.roll(ids_v[2 * j + 1], CAP, 1)
        )
    place256 = lax.broadcasted_iota(jnp.int32, (256, 512), 0)

    def mark(i, carry):
        first = pl.multiple_of(i * 256, 256)
        for j in range(SLOTS // 512):
            cols = slice(512 * j, 512 * j + 512)
            found = jnp.where(place256 == wanted[:, cols] - first, 1.0, 0.0)
            hits[pl.ds(first, 256), cols] = found.astype(BF)
        return carry

    lax.fori_loop(0, ROWS_DEV // 256, mark, 0)

    loads[1].wait()
    bottom_pre = jnp.dot(dense_ref[...], bw_ref[...], preferred_element_type=F32)
    lower = bottom_pre * jax.nn.sigmoid(bottom_pre)
    feats[:, 0:E] = lower.astype(BF)
    slope = silu_slope(bottom_pre)
    fgrad[:, 0:E] = slope
    for i in range(2, 5):
        loads[i].wait()
    pool = contract_first(hott_ref[...], hot_counts[...])
    feats[:, 2 * E : 3 * E] = pool.T.astype(BF)

    own.wait()
    for k in range(1, N_ROW):
        owner_k = to(k)
        remote(
            stage.at[k], rows_any.at[owner_k], row_send.at[k], row_recv.at[k], (rep, owner_k)
        ).wait_recv()
    read = pltpu.make_async_copy(rows_any, fetched, load_sem.at[1])
    read.start()
    read.wait()

    pool = contract_first(fetched[...].reshape(SLOTS, E), cold_counts[...])
    feats[:, E : 2 * E] = pool.T.astype(BF)
    slope = fgrad[:, 0:E]
    for h in range(H_TOP // 256):
        cols = slice(h * 256, (h + 1) * 256)
        weight = tw_ref[:, cols]
        pre = jnp.dot(feats[...], weight, preferred_element_type=F32)
        delta = (up_ref[:, cols].astype(F32) * silu_slope(pre)).astype(BF)
        deltas[:, cols] = delta
        term = contract_last(delta, weight)
        if h == 0:
            fgrad[...] = term
        else:
            fgrad[...] += term
    cold_back = fgrad[:, E : 2 * E].astype(BF)
    for s in range(SLOTS // 512):
        total = jnp.dot(
            cold_counts[s * 512 : (s + 1) * 512, :], cold_back, preferred_element_type=F32
        )
        slot[8 * s : 8 * s + 8] = total.astype(BF).reshape(8, CAP, E)

    feats_t[...] = feats[...].astype(F32).T.astype(BF)
    for h in range(H_TOP // 256):
        cols = slice(h * 256, (h + 1) * 256)
        top = jnp.dot(feats_t[...], deltas[:, cols], preferred_element_type=F32).astype(BF)
        w_ref[768 * h : 768 * h + 384, :] = top[:, 0:128]
        w_ref[768 * h + 384 : 768 * h + 768, :] = top[:, 128:256]
    bottom_delta = (fgrad[:, 0:E] * slope).astype(BF)
    w_ref[W_BOTTOM:W_HOT, :] = contract_first(dense_ref[...], bottom_delta).astype(BF)
    hot_back = fgrad[:, 2 * E : 3 * E].astype(BF)
    w_ref[W_HOT:W_USED, :] = jnp.dot(
        hot_counts[...], hot_back, preferred_element_type=F32
    ).astype(BF)
    w_ref[W_USED:W_ROWS, :] = jnp.zeros((W_ROWS - W_USED, E), BF)

    to_half = remote(
        w_ref.at[pl.ds(pl.multiple_of((1 - core) * W_C, W_C), W_C)], part_c, wc.at[0], wc.at[1],
        sibling,
    )
    to_half.start()

    sends = [None]
    for k in range(1, N_ROW):
        peer = to(k)
        sends.append(
            remote(slot.at[peer], arr_any.at[k], arr_send.at[k], arr_recv.at[k], (rep, peer))
        )

        sends[-1].start()
    own = pltpu.make_async_copy(slot.at[me], arr_any.at[0], load_sem.at[0])
    own.start()

    to_half.wait()

    def add_c(i, carry):
        rows = pl.ds(pl.multiple_of(i * 256, 256), 256)
        own_rows = pl.ds(pl.multiple_of(core * W_C + i * 256, 256), 256)
        half[rows, :] = (w_ref[own_rows, :].astype(F32) + part_c[rows, :].astype(F32)).astype(BF)
        return carry

    lax.fori_loop(0, W_C // 256, add_c, 0)
    to_y = []
    for k in range(1, NY):
        py = lax.rem(y + k, NY)
        to_y.append(
            remote(
                half.at[pl.ds(pl.multiple_of(py * W_Y, W_Y), W_Y)], part_y.at[k - 1],
                ry_send.at[k - 1], ry_recv.at[k - 1], y_peer(k),
            )
        )
        to_y[-1].start()
    for c in to_y:
        c.wait()
    total = half[pl.ds(pl.multiple_of(y * W_Y, W_Y), W_Y), :].astype(F32)
    for k in range(1, NY):
        total += part_y[k - 1].astype(F32)
    quarter[...] = total.astype(BF)
    to_x = []
    for k in range(1, NX):
        px = lax.rem(x + k, NX)
        to_x.append(
            remote(
                quarter.at[pl.ds(pl.multiple_of(px * W_X, W_X), W_X)], part_x.at[k - 1],
                rx_send.at[k - 1], rx_recv.at[k - 1], x_peer(k),
            )
        )
        to_x[-1].start()

    copies = []
    for part in range(4):
        for k in range(12 * part, 12 * part + 12):
            if k == 0:
                own.wait()
            else:
                sends[k].wait_recv()
        chunk = pl.ds(12 * part, 12)
        copies.append(
            pltpu.make_async_copy(arr_any.at[chunk], arr_v.at[chunk], arr_sem.at[part])
        )
        copies[-1].start()
    for c in copies:
        c.wait()

    def g_rows(c, j):
        return pl.ds(pl.multiple_of(c * G_C + j * G_Y, G_Y), G_Y)

    sign = 1 - 2 * core

    def ring(step):
        return lax.rem(y + step + NY, NY)

    def ring_peer(step):
        return (ring(step) * NC + core, me)

    def steps(s):
        return [4, s, -s, 2 * s, -2 * s, -3 * s, 3 * s, 0]

    def owned(c, j):
        values = arr_v[...].reshape(SLOTS, E)
        total = jnp.dot(hits[g_rows(c, j), :], values, preferred_element_type=F32)
        return total.astype(BF)

    def add_x():
        for c in to_x:
            c.wait()
        total = quarter[pl.ds(pl.multiple_of(x * W_X, W_X), W_X), :].astype(F32)
        for k in range(1, NX):
            total += part_x[k - 1].astype(F32)
        eighth[0:W_X, :] = total
        eighth[W_X : NZ * W_Z, :] = jnp.zeros((NZ * W_Z - W_X, E), F32)
        copies = []
        for k in range(1, NZ):
            pz = lax.rem(z + k, NZ)
            copies.append(
                remote(
                    eighth.at[pl.ds(pl.multiple_of(pz * W_Z, W_Z), W_Z)], part_z.at[k - 1],
                    rz_send.at[k - 1], rz_recv.at[k - 1], z_peer(k),
                )
            )
            copies[-1].start()
        return copies

    def add_z():
        for c in to_z:
            c.wait()
        total = eighth[pl.ds(pl.multiple_of(z * W_Z, W_Z), W_Z), :]
        for k in range(1, NZ):
            total += part_z[k - 1]
        summed[...] = total
        gath_z[0] = total
        copies = []
        for k in range(1, NZ):
            copies.append(
                remote(summed, gath_z.at[k], wz_send.at[k - 1], wz_recv.at[k - 1], z_peer(k))
            )
            copies[-1].start()
        return copies

    to_z = add_x()
    to_core = []

    def give(i):
        give_c[i] = owned(1 - core, ring(steps(-sign)[i]))
        to_core.append(
            remote(give_c.at[i], got_c.at[i], c_send.at[i], c_recv.at[i], sibling)
        )
        to_core[-1].start()

    give(0)
    give(1)
    over_y = []
    for i, step in enumerate(steps(sign)):
        if i + 2 < NY:
            give(i + 2)
        if i == 3:
            over_z = add_z()
        total = owned(core, ring(step)).astype(F32)
        to_core[i].wait_recv()
        total += got_c[i].astype(F32)
        if i == NY - 2:
            over_y[0].wait_recv()
            total += got_y[0].astype(F32)
        if i < NY - 1:
            mine[i] = total.astype(BF)
            peer = ring_peer(sign) if i == 0 else ring_peer(step)
            over_y.append(remote(mine.at[i], got_y.at[i], y_send.at[i], y_recv.at[i], peer))
            over_y[-1].start()

    for c in over_z:
        c.wait()

    def place(k, carry):
        owner_z = lax.rem(z - k + NZ, NZ)
        w_x[pl.ds(pl.multiple_of(owner_z * W_Z, W_Z), W_Z), :] = gath_z[k]
        return carry

    lax.fori_loop(0, NZ, place, 0)
    gath_y[y] = w_x[0:W_X, :].astype(BF)
    w_over_y = []
    for k in range(1, NY):
        w_over_y.append(
            remote(gath_y.at[y], gath_y.at[y], wy_send.at[k - 1], wy_recv.at[k - 1], y_peer(k))
        )
        w_over_y[-1].start()

    for i in range(1, NY - 1):
        over_y[i].wait_recv()
        total += got_y[i].astype(F32)
    final[...] = total.astype(BF)
    share_y = []
    onward = [3 * sign, sign, -sign, 2 * sign, -2 * sign, -3 * sign]
    for i, step in enumerate(onward):
        share_y.append(
            remote(
                final, cold_out.at[g_rows(core, y)], a_send.at[i], a_recv.at[i], ring_peer(step)
            )
        )
        share_y[-1].start()
    share_c = [
        remote(final, cold_out.at[g_rows(core, y)], b_send.at[0], b_recv.at[0], sibling)
    ]
    share_c[0].start()
    cold_out[g_rows(core, y), :] = final[...]

    def forward(i, step):
        rows = cold_out.at[g_rows(core, ring(-step))]
        share_c.append(remote(rows, rows, b_send.at[i], b_recv.at[i], sibling))
        share_c[-1].start()

    for c in w_over_y:
        c.wait()
    w_over_x = []
    for k in range(1, NX):
        w_over_x.append(
            remote(gath_y, gath_x.at[x], wx_send.at[k - 1], wx_recv.at[k - 1], x_peer(k))
        )
        w_over_x[-1].start()
    gath_x[x] = gath_y[...]

    share_y[0].wait_recv()
    rows = cold_out.at[g_rows(core, ring(-3 * sign))]
    share_y.append(remote(rows, rows, a_send.at[6], a_recv.at[6], ring_peer(sign)))
    share_y[6].start()
    for i, step in enumerate(onward):
        if i > 0:
            share_y[i].wait_recv()
        forward(i + 1, step)
    for c in w_over_x:
        c.wait()
    w_over_c = remote(gath_x, w_out.at[core], wc_sem.at[0], wc_sem.at[1], sibling)
    w_over_c.start()
    w_out[core] = gath_x[...]
    share_y[6].wait_recv()
    forward(7, 4)

    for k in range(1, N_ROW):
        asks[k].wait_send()
        sends[k].wait_send()
        remote(
            stage.at[k], rows_any.at[me], row_send.at[k], row_recv.at[k], (rep, to(k))
        ).wait_send()
    for c in to_core + over_y + share_y:
        c.wait_send()
    for c in share_c:
        c.wait()
    w_over_c.wait()


def step(requests, cold_bags, hot_bags, bottom_weight, table, dense, upstream, top_weight, hot):
    dma = pltpu.SemaphoreType.DMA
    hbm = pl.BlockSpec(memory_space=pl.ANY)
    v = pltpu.VMEM
    rows = (N_ROW, CAP, E)
    return pl.pallas_call(
        step_kernel,
        out_shape=(
            jax.ShapeDtypeStruct((ROWS_DEV, E), BF),
            jax.ShapeDtypeStruct((NC, NX, NY, W_X, E), BF),
            jax.ShapeDtypeStruct(rows, BF),
            jax.ShapeDtypeStruct(rows, BF),
        ),
        in_specs=[vmem()] * 4 + [hbm] * 5,
        out_specs=(vmem(), vmem(), hbm, hbm),
        scratch_shapes=[
            v((N_ROW, 1, 128), jnp.int32),
            v((N_ROW, 1, 128), jnp.int32),
            pltpu.SMEM((N_ROW, 1, 128), jnp.int32),
            v((ROWS_DEV, E), BF),
            v((ROWS_DEV, E), F32),
            v((CAP, E), F32),
            v(rows, BF),
            v(rows, BF),
            v((B_DEV, D_BOT), BF),
            v((B_DEV, H_TOP), BF),
            v((3 * E, H_TOP), BF),
            v((HOT, E), BF),
            v((SLOTS, B_DEV), BF),
            v((HOT, B_DEV), BF),
            v((B_DEV, 3 * E), BF),
            v((3 * E, B_DEV), BF),
            v((B_DEV, H_TOP), BF),
            v((B_DEV, 3 * E), F32),
            v(rows, BF),
            v((W_ROWS, E), BF),
            v(rows, BF),
            v((1, SLOTS), jnp.int32),
            v((ROWS_DEV, SLOTS), BF),
            v((NY, G_Y, E), BF),
            v((W_C, E), BF),
            v((W_C, E), BF),
            v((NX - 1, W_X, E), BF),
            v((W_Y, E), BF),
            v((NY - 1, W_Y, E), BF),
            v((NZ * W_Z, E), F32),
            v((NZ - 1, W_Z, E), F32),
            v((W_Z, E), F32),
            v((NY, G_Y, E), BF),
            v((NY - 1, G_Y, E), BF),
            v((NY - 1, G_Y, E), BF),
            v((G_Y, E), BF),
            v((NZ, W_Z, E), F32),
            v((NZ * W_Z, E), F32),
            v((NX, NY, W_X, E), BF),
            v((NY, W_X, E), BF),
            dma((5,)),
        ]
        + [dma((N_ROW,))] * 6
        + [dma((4,)), dma((2,))]
        + [dma((NX - 1,))] * 2
        + [dma((NY - 1,))] * 2
        + [dma((NZ - 1,))] * 2
        + [dma((NY,))] * 2
        + [dma((NY - 1,))] * 4
        + [dma((NY,))] * 2
        + [dma((NZ - 1,))] * 2
        + [dma((NY - 1,))] * 2
        + [dma((NX - 1,))] * 2
        + [dma((2,))],
        compiler_params=pltpu.CompilerParams(
            collective_id=0, has_side_effects=True, vmem_limit_bytes=VMEM_LIMIT
        ),
        name="step",
    )(requests, cold_bags, hot_bags, bottom_weight, table, dense, upstream, top_weight, hot)


def widen_kernel(cold_ref, w_ref, top_out, bottom_out, hot_out, cold_out):
    for c in range(NC):
        for yy in range(NY):
            for xx in range(NX):
                row = c * W_C + yy * W_Y + xx * W_X
                values = w_ref[c, xx, yy].astype(F32)
                if row < W_BOTTOM:
                    col, first = row // (3 * E), row % (3 * E)
                    top_out[first : first + W_X, col * E : (col + 1) * E] = values
                elif row < W_HOT:
                    bottom_out[row - W_BOTTOM : row - W_BOTTOM + W_X, :] = values
                elif row < W_USED:
                    hot_out[row - W_HOT : row - W_HOT + W_X, :] = values
    cold_out[...] = cold_ref[...].astype(F32)


def widen(cold, w):
    return pl.pallas_call(
        widen_kernel,
        out_shape=(
            jax.ShapeDtypeStruct((3 * E, H_TOP), F32),
            jax.ShapeDtypeStruct((D_BOT, E), F32),
            jax.ShapeDtypeStruct((HOT, E), F32),
            jax.ShapeDtypeStruct((ROWS_DEV, E), F32),
        ),
        in_specs=[vmem()] * 2,
        out_specs=(vmem(),) * 4,
        compiler_params=pltpu.CompilerParams(vmem_limit_bytes=VMEM_LIMIT),
        name="widen",
    )(cold, w)


def local(
    dense_act,
    upstream,
    bottom_weight,
    top_weight,
    hot_table,
    cold_table,
    hot_bags,
    cold_bags,
    requests,
):
    cold, w, _, _ = step(
        requests.reshape(N_ROW, 1, CAP), cold_bags.T, hot_bags.T, bottom_weight, cold_table,
        dense_act, upstream, top_weight, hot_table,
    )
    return widen(cold, w)


def solution(mesh):
    placed = (
        P(("rep", "row"), None),
        P(("rep", "row"), None),
        P(),
        P(),
        P(),
        P("row", None),
        P(("rep", "row"), None),
        P(("rep", "row"), None),
        P("rep", "row", None, None),
    )
    return jax.shard_map(
        local,
        mesh=mesh,
        in_specs=placed,
        out_specs=(P(), P(), P(), P("row", None)),
        check_vma=False,
    )
```
